32 devices in a mesh: row: 4 (over x, core), col: 8 (over z, y).
Axes of the slice: x: 2, y: 2, z: 4, core: 2. Of those that a mesh axis runs over, the one named last changes fastest.
Arguments:
- blocks: float32 [4, 8, 4, 128, 128], P('row', 'col')
- block_rows: int32 [4, 8, 4], P('row', 'col'), may hold values from 0 to 31, as said below
- block_cols: int32 [4, 8, 4], P('row', 'col'), may hold values from 0 to 7
- counts: int32 [4, 8], P('row', 'col'), may hold values from 2 to 4, as said below
- x_prev: float32 [8192], P('col'), may hold values from 0 to 1
- y_prev: float32 [16384], P('row'), may hold values from -6 to 6
- cost: float32 [8192], P('col'), may hold values from -6 to 6
- rhs: float32 [16384], P('row'), may hold values from -6 to 6
- upper: float32 [8192], P('col'), may hold values from 0.5 to 4
- steps: float32 [2], replicated, may hold values from 0.1 to 0.4
Outputs:
- x_new: float32 [8192], P('col')
- y_new: float32 [16384], P('row')
- stats: float32 [3], replicated
The draws below stay inside these ranges and needn't reach their ends.
Inputs may be any that keep to these rules, and one draw needn't show every extreme that they name: `block_rows`: pairs of block row and block column may repeat within a device. `counts`: stored blocks at positions from the count on are padding and are not part of the matrix; some device holds 4 live blocks in every draw.
All inputs are finite; a program needn't handle non-finite values.
Results may differ from the reference program's by a relative error of at most 0.00011.
Values sent between devices are 32-bit elements; how exact they have to be, the bound alone decides.
No kernel may reach another device: no remote copies, remote signals or barrier semaphores. Data moves between devices by JAX's collectives and lax.ppermute only.
A program may use at most 64 MiB of HBM per device.

```python
import math
import jax
import jax.numpy as jnp
from jax import lax

BS = 128
RB = 32
CB = 8
NBD = 4
NRG = 4
NCG = 8
M = 16384
N = 8192


def pattern(key):
    rows = jax.random.randint(jax.random.fold_in(key, 11), (NRG, NCG, NBD), 0, RB)
    cols = jax.random.randint(jax.random.fold_in(key, 12), (NRG, NCG, NBD), 0, CB)
    return (rows, cols)


def draw_block_rows(key, part):
    return pattern(key)[0].astype(jnp.int32)


def draw_block_cols(key, part):
    return pattern(key)[1].astype(jnp.int32)


def draw_counts(key, part):
    base = jax.random.randint(jax.random.fold_in(key, 21), (NRG * NCG,), NBD // 2, NBD + 1)
    pick = jax.random.randint(jax.random.fold_in(key, 22), (), 0, NRG * NCG)
    full = jnp.where(jnp.arange(NRG * NCG) == pick, NBD, base)
    return full.reshape(NRG, NCG).astype(jnp.int32)


def draw_blocks(key, part):
    rows, cols = pattern(key)
    grow = jnp.arange(NRG)[:, None, None] * RB + rows
    gcol = jnp.arange(NCG)[None, :, None] * CB + cols
    low = jnp.log(0.05)
    high = jnp.log(2.0)
    entries = jax.random.normal(jax.random.fold_in(key, 31), (NRG, NCG, NBD, BS, BS), jnp.float32)
    row_scale = jnp.exp(jax.random.uniform(jax.random.fold_in(key, 32), (NRG * RB, BS), jnp.float32, low, high))
    col_scale = jnp.exp(jax.random.uniform(jax.random.fold_in(key, 33), (NCG * CB, BS), jnp.float32, low, high))
    return (entries * row_scale[grow][..., :, None] * col_scale[gcol][..., None, :]).astype(jnp.float32)


def levels(own_key, shape, shards, low, top_value):
    gain, own = 1.0, jax.random.fold_in(own_key, 6)
    for position, shards_of in shards:
        heights = jnp.exp(jax.random.uniform(jax.random.fold_in(own, position), (shards_of,), jnp.float32, low / len(shards), top_value / len(shards)))
        gain = gain * jnp.repeat(heights, shape[position] // shards_of).reshape([-1 if axis == position else 1 for axis in range(len(shape))])
    return gain


def normal_values(stream_key, shape, deviation, bound, split=(), kind=jnp.bfloat16):
    result = jax.random.normal(stream_key, shape, jnp.float32) * deviation
    if len(split) > 0:
        result = levels(stream_key, shape, split, -0.22, 0.18) * result
    return jnp.clip(result, min=-bound, max=bound).astype(kind)


def setup_inputs(seed: int = 0) -> dict:
    splits = jax.random.split(jax.random.key(seed), 11)
    return {
        "blocks": draw_blocks(jax.random.fold_in(splits[10], 71), 0),
        "block_rows": draw_block_rows(jax.random.fold_in(splits[10], 71), 0),
        "block_cols": draw_block_cols(jax.random.fold_in(splits[10], 71), 0),
        "counts": draw_counts(jax.random.fold_in(splits[10], 71), 0),
        "x_prev": jnp.clip(1.0 * jax.random.uniform(splits[4], (N,), jnp.float32) ** levels(splits[4], (N,), ((0, 8),), -0.2, 0.2), 0.0, 1.0),
        "y_prev": normal_values(splits[5], (M,), 1.0, 6.0, ((0, 4),), jnp.float32),
        "cost": normal_values(splits[6], (N,), 1.0, 6.0, ((0, 8),), jnp.float32),
        "rhs": normal_values(splits[7], (M,), 1.0, 6.0, ((0, 4),), jnp.float32),
        "upper": jnp.clip(jnp.exp(math.log(4.0) - 2.0794415 * jax.random.uniform(splits[8], (N,), jnp.float32) ** levels(splits[8], (N,), ((0, 8),), -0.2, 0.2)), 0.5, 4.0),
        "steps": jnp.clip(jax.random.uniform(splits[9], (2,), jnp.float32, 0.1, 0.4), 0.1, 0.4),
    }


def reference(blocks, block_rows, block_cols, counts, x_prev, y_prev, cost, rhs, upper, steps):
    nbd = blocks.shape[2]
    live = (jnp.arange(nbd, dtype=jnp.int32)[None, None, :] < counts[:, :, None]).astype(jnp.float32).reshape(-1)
    grow = (jnp.arange(NRG, dtype=jnp.int32)[:, None, None] * RB + block_rows).reshape(-1)
    gcol = (jnp.arange(NCG, dtype=jnp.int32)[None, :, None] * CB + block_cols).reshape(-1)
    flat = blocks.reshape(-1, BS, BS)
    rpeak = lax.optimization_barrier(jnp.max(jnp.abs(flat), axis=2)) * live[:, None]
    cpeak = lax.optimization_barrier(jnp.max(jnp.abs(flat), axis=1)) * live[:, None]
    rowmax = jnp.maximum(jax.ops.segment_max(rpeak, grow, num_segments=NRG * RB), 0.0).reshape(-1)
    colmax = jnp.maximum(jax.ops.segment_max(cpeak, gcol, num_segments=NCG * CB), 0.0).reshape(-1)
    row_scale = 1.0 / jnp.sqrt(jnp.maximum(rowmax, 0.5))
    col_scale = 1.0 / jnp.sqrt(jnp.maximum(colmax, 0.5))

    def forward(vecs):
        count = vecs.shape[0]
        picked = (vecs * col_scale[None, :]).reshape(count, NCG * CB, BS)[:, gcol]
        prod = jnp.einsum('kij,vkj->kvi', flat, picked, precision=lax.Precision.HIGHEST) * live[:, None, None]
        summed = jax.ops.segment_sum(prod, grow, num_segments=NRG * RB)
        return jnp.transpose(summed, (1, 0, 2)).reshape(count, -1) * row_scale[None, :]

    def backward(vec):
        picked = (vec * row_scale).reshape(NRG * RB, BS)[grow]
        prod = jnp.einsum('kij,ki->kj', flat, picked, precision=lax.Precision.HIGHEST) * live[:, None]
        return jax.ops.segment_sum(prod, gcol, num_segments=NCG * CB).reshape(-1) * col_scale
    cost_s = col_scale * cost
    rhs_s = row_scale * rhs
    upper_s = upper / col_scale
    eta = steps[0]
    omega = steps[1]
    tau = eta / omega
    sigma = eta * omega
    grad = cost_s - backward(y_prev)
    x_new = jnp.clip(x_prev - tau * grad, 0.0, upper_s)
    delta_x = x_new - x_prev
    both = forward(jnp.stack([x_new, delta_x]))
    ax_new = both[0]
    adx = both[1]
    y_new = y_prev + sigma * (rhs_s - ax_new - adx)
    delta_y = y_new - y_prev
    reduced = cost_s - backward(y_new)
    resid = rhs_s - ax_new
    dx2 = jnp.sum(delta_x * delta_x)
    cx = jnp.sum(cost_s * x_new)
    uneg = jnp.sum(upper_s * jnp.maximum(-reduced, 0.0))
    dy2 = jnp.sum(delta_y * delta_y)
    adx2 = jnp.sum(adx * adx)
    res2 = jnp.sum(resid * resid)
    by = jnp.sum(rhs_s * y_new)
    movement = 0.5 * omega * dx2 + 0.5 / omega * dy2
    stats = jnp.stack([jnp.sqrt(res2 / M), (cx - by + uneg) / N, movement / jnp.sqrt(adx2 * dy2 + 1e-06)])
    return (x_new, y_new, stats)
```

```python
import functools

import jax
import jax.numpy as jnp
from jax import lax
from jax.experimental import pallas as pl
from jax.experimental.pallas import tpu as pltpu
from jax.sharding import PartitionSpec as P

F32 = jnp.float32
VMEM = pl.BlockSpec(memory_space=pltpu.VMEM)
SMEM = pl.BlockSpec(memory_space=pltpu.SMEM)
LIMIT = 40 * 1024 * 1024


def up(n, m):
    return -(-n // m) * m


def iota(shape, dim):
    return lax.broadcasted_iota(jnp.int32, shape, dim)


def rows_of(rows, bsz):
    lane = iota((bsz, bsz), 1)
    cols = jnp.zeros((bsz, bsz), F32)
    for k, col in enumerate(rows):
        cols = jnp.where(lane == k, col, cols)
    return cols.T


def peaks_kernel(nbd, blocks, y, rhs, brow, bcol, count, p1, bulk):
    bsz = blocks.shape[1]
    hp = p1.shape[1]
    rb = y.shape[0]
    peaks = []
    for k in range(nbd):
        a = blocks[k * bsz : (k + 1) * bsz, :]
        bulk[k * bsz : (k + 1) * bsz, :] = a
        peaks.append(jnp.max(jnp.abs(a), axis=1, keepdims=True))
    rows = rows_of(peaks, bsz)[:hp]
    sub = iota((hp, bsz), 0)
    base = nbd * bsz
    bulk[base : base + rb, :] = y[...]
    bulk[base + rb : base + 2 * rb, :] = rhs[...]
    ch = bulk.shape[0] - base - 2 * rb
    csub = iota((ch, bsz), 0)
    cols = jnp.zeros((ch, bsz), F32)
    for k in range(nbd):
        code = jnp.where(k < count[0], brow[k], -1).astype(F32)
        rows = jnp.where(sub == nbd + k, code, rows)
        cols = jnp.where(csub == k, bcol[k].astype(F32), cols)
    bulk[base + 2 * rb :, :] = cols
    p1[...] = jnp.broadcast_to(rows[None], p1.shape)


def backward(nbd, R, C, origins, slots, g1, w_ref, wr, part, cb):
    me_r = lax.axis_index("row")
    me_c = lax.axis_index("col")
    bsz = slots[0].shape[1]
    rb = w_ref.shape[0] // R
    rio = iota((rb, bsz), 0).astype(F32)
    cio = iota((cb, bsz), 0).astype(F32)
    for s, slot in enumerate(slots):
        q = origins(me_r, s)
        w = w_ref[pl.ds(pl.multiple_of(q * rb, rb), rb), :]
        tile = g1[q * C + me_c]
        for k in range(nbd):
            pick = jnp.where(rio == tile[nbd + k : nbd + k + 1, :], w, 0.0)
            wr[s * nbd + k : s * nbd + k + 1, :] = jnp.sum(pick, axis=0, keepdims=True)
    wt = wr[...].T
    for s, slot in enumerate(slots):
        q = origins(me_r, s)
        cols = slot[slot.shape[0] - up(nbd, 8) :, :]
        total = jnp.zeros((cb, bsz), F32)
        for k in range(nbd):
            i = s * nbd + k
            prod = jnp.sum(
                slot[k * bsz : (k + 1) * bsz, :] * wt[:, i : i + 1], axis=0, keepdims=True
            )
            total += jnp.where(cio == cols[k : k + 1, :], prod, 0.0)
        part[q] = total
    out = part[0]
    for q in range(1, R):
        out += part[q]
    return out


def primal_kernel(nbd, R, C, origins, g1, *refs):
    slots = refs[:R]
    x_prev, cost, upper, steps, x_new, dr, dc, p3, w_ref, wr, part = refs[R:]
    me_r = lax.axis_index("row")
    me_c = lax.axis_index("col")
    bsz = x_prev.shape[1]
    cb = x_prev.shape[0]
    rb = dr.shape[0] // R
    base = nbd * bsz
    rio = iota((rb, bsz), 0).astype(F32)
    cio = iota((cb, bsz), 0).astype(F32)
    wr[...] = jnp.zeros_like(wr)
    for q in range(R):

        def body(c, acc):
            tile = g1[q * C + c]
            for k in range(nbd):
                hit = rio == tile[nbd + k : nbd + k + 1, :]
                acc = jnp.maximum(acc, jnp.where(hit, tile[k : k + 1, :], 0.0))
            return acc

        peak = lax.fori_loop(0, C, body, jnp.zeros((rb, bsz), F32), unroll=min(C, 8))
        dr[q * rb : (q + 1) * rb, :] = 1.0 / jnp.sqrt(jnp.maximum(peak, 0.5))
    colmax = jnp.zeros((cb, bsz), F32)
    for s, slot in enumerate(slots):
        q = origins(me_r, s)
        tile = g1[q * C + me_c]
        cols = slot[slot.shape[0] - up(nbd, 8) :, :]
        at = pl.ds(pl.multiple_of(q * rb, rb), rb)
        w_ref[at, :] = dr[at, :] * slot[base : base + rb, :]
        for k in range(nbd):
            a = slot[k * bsz : (k + 1) * bsz, :]
            cp = jnp.max(jnp.abs(a), axis=0, keepdims=True)
            hit = (cio == cols[k : k + 1, :]) & (tile[nbd + k : nbd + k + 1, :] >= 0.0)
            colmax = jnp.maximum(colmax, jnp.where(hit, cp, 0.0))
    scale = 1.0 / jnp.sqrt(jnp.maximum(colmax, 0.5))
    dc[...] = scale
    got = backward(nbd, R, C, origins, slots, g1, w_ref, wr, part, cb)
    tau = steps[0] / steps[1]
    grad = scale * cost[...] - got * scale
    xp = x_prev[...]
    xn = jnp.clip(xp - tau * grad, 0.0, upper[...] / scale)
    x_new[...] = xn
    v1 = scale * xn
    v2 = scale * (xn - xp)
    own = slots[0]
    cols = own[own.shape[0] - up(nbd, 8) :, :]
    res = []
    for k in range(nbd):
        a = own[k * bsz : (k + 1) * bsz, :]
        hit = cio == cols[k : k + 1, :]
        for v in (v1, v2):
            vk = jnp.sum(jnp.where(hit, v, 0.0), axis=0, keepdims=True)
            res.append(jnp.sum(a * vk, axis=1, keepdims=True))
    rows = rows_of(res, bsz)[: p3.shape[1]]
    p3[...] = jnp.broadcast_to(rows[None], p3.shape)


def dual_kernel(nbd, R, C, origins, g1, g3, *refs):
    slots = refs[:R]
    x_prev, cost, upper, steps, x_new, dr, dc, y_new, p4, dual, w_ref, wr, part = refs[R:]
    me_r = lax.axis_index("row")
    bsz = x_prev.shape[1]
    cb = x_prev.shape[0]
    rb = dr.shape[0] // R
    base = nbd * bsz
    rio = iota((rb, bsz), 0).astype(F32)
    wr[...] = jnp.zeros_like(wr)
    sigma = steps[0] * steps[1]
    dr_all = []
    for s, slot in enumerate(slots):
        q = origins(me_r, s)
        at = pl.ds(pl.multiple_of(q * rb, rb), rb)

        def body(c, acc):
            one, two = acc
            tile = g1[q * C + c]
            got = g3[q * C + c]
            for k in range(nbd):
                hit = rio == tile[nbd + k : nbd + k + 1, :]
                one = one + jnp.where(hit, got[2 * k : 2 * k + 1, :], 0.0)
                two = two + jnp.where(hit, got[2 * k + 1 : 2 * k + 2, :], 0.0)
            return one, two

        zero = jnp.zeros((rb, bsz), F32)
        ax, adx = lax.fori_loop(0, C, body, (zero, zero), unroll=min(C, 8))
        scale = dr[at, :]
        ax = ax * scale
        adx = adx * scale
        bs = scale * slot[base + rb : base + 2 * rb, :]
        yp = slot[base : base + rb, :]
        yn = yp + sigma * (bs - ax - adx)
        if s == 0:
            y_new[...] = yn
        w_ref[at, :] = scale * yn
        dy = yn - yp
        resid = bs - ax
        for i, term in enumerate((dy * dy, adx * adx, resid * resid, bs * yn)):
            part[q, i : i + 1, :] = jnp.sum(term, axis=0, keepdims=True)
    sums = part[0, :4, :]
    for q in range(1, R):
        sums += part[q, :4, :]
    dual[...] = jnp.broadcast_to(jnp.sum(sums, axis=1, keepdims=True), dual.shape)
    got = backward(nbd, R, C, origins, slots, g1, w_ref, wr, part, cb)
    scale = dc[...]
    cs = scale * cost[...]
    reduced = cs - got * scale
    us = upper[...] / scale
    xn = x_new[...]
    dx = xn - x_prev[...]
    lane = iota((1, bsz), 1)
    out = jnp.zeros((1, bsz), F32)
    for i, term in enumerate((dx * dx, cs * xn, us * jnp.maximum(-reduced, 0.0))):
        out = jnp.where(lane == i, jnp.sum(term), out)
    p4[...] = jnp.broadcast_to(out, p4.shape)


def stats_kernel(total_rows, total_cols, g4, dual, steps, stats):
    bsz = g4.shape[1]
    primal = jnp.sum(g4[...], axis=0, keepdims=True)
    lane = iota((1, bsz), 1)

    def pick(i):
        return jnp.sum(jnp.where(lane == i, primal, 0.0), axis=1, keepdims=True)

    dx2, cx, uneg = (jnp.broadcast_to(pick(i), (1, bsz)) for i in range(3))
    dy2, adx2, res2, by = (dual[i : i + 1, :] for i in range(4))
    omega = steps[1]
    movement = 0.5 * omega * dx2 + 0.5 / omega * dy2
    first = jnp.sqrt(res2 / total_rows)
    second = (cx - by + uneg) / total_cols
    third = movement / jnp.sqrt(adx2 * dy2 + 1e-06)
    out = jnp.where(lane == 0, first, jnp.where(lane == 1, second, third))
    stats[...] = out[:, : stats.shape[1]]


def shards(blocks, block_rows, block_cols, counts, x_prev, y_prev, cost, rhs, upper, steps):
    R = lax.axis_size("row")
    C = lax.axis_size("col")
    ndev = R * C
    nbd, bsz = blocks.shape[2], blocks.shape[3]
    rb = y_prev.shape[0] // bsz
    cb = x_prev.shape[0] // bsz
    hp = up(2 * nbd, 8)
    flat = blocks.reshape(nbd * bsz, bsz)
    y2, rhs2 = y_prev.reshape(rb, bsz), rhs.reshape(rb, bsz)
    x2, cost2, upper2 = (v.reshape(cb, bsz) for v in (x_prev, cost, upper))
    params = pltpu.CompilerParams(vmem_limit_bytes=LIMIT)
    bulk_rows = nbd * bsz + 2 * rb + up(nbd, 8)
    p1, bulk = pl.pallas_call(
        functools.partial(peaks_kernel, nbd),
        out_shape=(
            jax.ShapeDtypeStruct((ndev, hp, bsz), F32),
            jax.ShapeDtypeStruct((bulk_rows, bsz), F32),
        ),
        in_specs=[VMEM] * 3 + [SMEM] * 3,
        out_specs=(VMEM, VMEM),
        compiler_params=params,
        name="peaks",
    )(flat, y2, rhs2, block_rows.reshape(nbd), block_cols.reshape(nbd), counts.reshape(1))

    def spread(v):
        return lax.all_to_all(v, ("row", "col"), 0, 0, tiled=True)

    slots, ids = [bulk], [0]
    if R & (R - 1) == 0:
        step = R // 2
        while step:
            perm = [(i, i ^ step) for i in range(R)]
            slots += [lax.ppermute(b, "row", perm) for b in slots]
            ids += [i ^ step for i in ids]
            step //= 2

        def origins(me, s):
            return me ^ ids[s] if ids[s] else me

    else:
        for step in range(1, R):
            slots.append(lax.ppermute(bulk, "row", [(i, (i - step) % R) for i in range(R)]))

        def origins(me, s):
            return lax.rem(me + s, R)

    g1 = spread(p1)
    scratch = [
        pltpu.VMEM((R * rb, bsz), F32),
        pltpu.VMEM((up(R * nbd, bsz), bsz), F32),
        pltpu.VMEM((R, cb, bsz), F32),
    ]
    x_new, dr, dc, p3 = pl.pallas_call(
        functools.partial(primal_kernel, nbd, R, C, origins),
        out_shape=(
            jax.ShapeDtypeStruct((cb, bsz), F32),
            jax.ShapeDtypeStruct((R * rb, bsz), F32),
            jax.ShapeDtypeStruct((cb, bsz), F32),
            jax.ShapeDtypeStruct((ndev, hp, bsz), F32),
        ),
        in_specs=[VMEM] * (1 + R + 3) + [SMEM],
        out_specs=(VMEM,) * 4,
        scratch_shapes=scratch,
        compiler_params=params,
        name="primal",
    )(g1, *slots, x2, cost2, upper2, steps)
    g3 = spread(p3)
    y_new, p4, dual = pl.pallas_call(
        functools.partial(dual_kernel, nbd, R, C, origins),
        out_shape=(
            jax.ShapeDtypeStruct((rb, bsz), F32),
            jax.ShapeDtypeStruct((C, bsz), F32),
            jax.ShapeDtypeStruct((4, bsz), F32),
        ),
        in_specs=[VMEM] * (2 + R + 3) + [SMEM] + [VMEM] * 3,
        out_specs=(VMEM,) * 3,
        scratch_shapes=scratch,
        compiler_params=params,
        name="dual",
    )(g1, g3, *slots, x2, cost2, upper2, steps, x_new, dr, dc)
    g4 = lax.all_to_all(p4, "col", 0, 0, tiled=True)
    stats = pl.pallas_call(
        functools.partial(
            stats_kernel, float(y_prev.shape[0] * R), float(x_prev.shape[0] * C)
        ),
        out_shape=jax.ShapeDtypeStruct((1, 3), F32),
        in_specs=[VMEM, VMEM, SMEM],
        out_specs=VMEM,
        compiler_params=params,
        name="stats",
    )(g4, dual, steps)
    return (x_new.reshape(-1), y_new.reshape(-1), stats.reshape(-1))


def solution(mesh):
    placed = (
        P("row", "col", None, None, None),
        P("row", "col", None),
        P("row", "col", None),
        P("row", "col"),
        P("col"),
        P("row"),
        P("col"),
        P("row"),
        P("col"),
        P(),
    )
    return jax.shard_map(
        shards, mesh=mesh, in_specs=placed, out_specs=(P("col"), P("row"), P()), check_vma=False
    )
```

```python
import functools

import jax
import jax.numpy as jnp
from jax import lax
from jax.experimental import pallas as pl
from jax.experimental.pallas import tpu as pltpu
from jax.sharding import PartitionSpec as P

F32 = jnp.float32
VMEM = pl.BlockSpec(memory_space=pltpu.VMEM)
SMEM = pl.BlockSpec(memory_space=pltpu.SMEM)
HBM = pl.BlockSpec(memory_space=pltpu.HBM)
LIMIT = 40 * 1024 * 1024


def up(n, m):
    return -(-n // m) * m


def iota(shape, dim):
    return lax.broadcasted_iota(jnp.int32, shape, dim)


def rows_of(rows, bsz):
    lane = iota((bsz, bsz), 1)
    cols = jnp.zeros((bsz, bsz), F32)
    for k, col in enumerate(rows):
        cols = jnp.where(lane == k, col, cols)
    return cols.T


def peaks_kernel(nbd, blocks, y, rhs, x, cost, upper, brow, bcol, steps, count, p1, bulk, aux, *scratch):
    s_row, s_col, s_steps, sems = scratch
    bsz = bulk.shape[1]
    hp = p1.shape[1]
    rb = y.shape[0]
    cb = x.shape[0]
    base = nbd * bsz
    pairs = [
        (brow, s_row),
        (bcol, s_col),
        (steps, s_steps),
        (y, bulk.at[base : base + rb]),
        (rhs, bulk.at[base + rb : base + 2 * rb]),
        (x, aux.at[:cb]),
        (cost, aux.at[cb : 2 * cb]),
        (upper, aux.at[2 * cb : 3 * cb]),
    ]
    loads = [
        pltpu.make_async_copy(blocks.at[k], bulk.at[k * bsz : (k + 1) * bsz], sems.at[k])
        for k in range(nbd)
    ]
    rest = [pltpu.make_async_copy(a, b, sems.at[nbd + i]) for i, (a, b) in enumerate(pairs)]
    for copy in loads + rest:
        copy.start()
    peaks = []
    for k in range(nbd):
        loads[k].wait()
        a = bulk[k * bsz : (k + 1) * bsz, :]
        peaks.append(jnp.max(jnp.abs(a), axis=1, keepdims=True))
    rows = rows_of(peaks, bsz)[:hp]
    for copy in rest:
        copy.wait()
    sub = iota((hp, bsz), 0)
    ch = bulk.shape[0] - base - 2 * rb
    csub = iota((ch, bsz), 0)
    cols = jnp.zeros((ch, bsz), F32)
    for k in range(nbd):
        code = jnp.where(k < count[0, 0], s_row[0, 0, k], -1).astype(F32)
        rows = jnp.where(sub == nbd + k, code, rows)
        cols = jnp.where(csub == k, s_col[0, 0, k].astype(F32), cols)
    bulk[base + 2 * rb :, :] = cols
    asub = iota((8, bsz), 0)
    aux[3 * cb :, :] = jnp.where(asub == 0, s_steps[0], s_steps[1])
    p1[...] = jnp.broadcast_to(rows[None], p1.shape)


def backward(nbd, R, C, origins, slots, g1, w_ref, wr, part, cb):
    me_r = lax.axis_index("row")
    me_c = lax.axis_index("col")
    bsz = slots[0].shape[1]
    rb = w_ref.shape[0] // R
    rio = iota((rb, bsz), 0).astype(F32)
    cio = iota((cb, bsz), 0).astype(F32)
    for s, slot in enumerate(slots):
        q = origins(me_r, s)
        w = w_ref[pl.ds(pl.multiple_of(q * rb, rb), rb), :]
        tile = g1[q * C + me_c]
        for k in range(nbd):
            pick = jnp.where(rio == tile[nbd + k : nbd + k + 1, :], w, 0.0)
            wr[s * nbd + k : s * nbd + k + 1, :] = jnp.sum(pick, axis=0, keepdims=True)
    wt = wr[...].T
    for s, slot in enumerate(slots):
        q = origins(me_r, s)
        cols = slot[slot.shape[0] - up(nbd, 8) :, :]
        total = jnp.zeros((cb, bsz), F32)
        for k in range(nbd):
            i = s * nbd + k
            prod = jnp.sum(
                slot[k * bsz : (k + 1) * bsz, :] * wt[:, i : i + 1], axis=0, keepdims=True
            )
            total += jnp.where(cio == cols[k : k + 1, :], prod, 0.0)
        part[q] = total
    out = part[0]
    for q in range(1, R):
        out += part[q]
    return out


def primal_kernel(nbd, R, C, origins, g1, *refs):
    slots = refs[:R]
    aux, x_new, dr, dc, p3, w_ref, wr, part = refs[R:]
    me_r = lax.axis_index("row")
    me_c = lax.axis_index("col")
    cb, bsz = x_new.shape
    x_prev, cost, upper = (aux.at[i * cb : (i + 1) * cb] for i in range(3))
    eta, omega = (aux[3 * cb + i : 3 * cb + i + 1, :] for i in range(2))
    rb = dr.shape[0] // R
    base = nbd * bsz
    rio = iota((rb, bsz), 0).astype(F32)
    cio = iota((cb, bsz), 0).astype(F32)
    wr[...] = jnp.zeros_like(wr)
    for q in range(R):

        def body(c, acc):
            tile = g1[q * C + c]
            for k in range(nbd):
                hit = rio == tile[nbd + k : nbd + k + 1, :]
                acc = jnp.maximum(acc, jnp.where(hit, tile[k : k + 1, :], 0.0))
            return acc

        peak = lax.fori_loop(0, C, body, jnp.zeros((rb, bsz), F32), unroll=min(C, 8))
        dr[q * rb : (q + 1) * rb, :] = 1.0 / jnp.sqrt(jnp.maximum(peak, 0.5))
    colmax = jnp.zeros((cb, bsz), F32)
    for s, slot in enumerate(slots):
        q = origins(me_r, s)
        tile = g1[q * C + me_c]
        cols = slot[slot.shape[0] - up(nbd, 8) :, :]
        at = pl.ds(pl.multiple_of(q * rb, rb), rb)
        w_ref[at, :] = dr[at, :] * slot[base : base + rb, :]
        for k in range(nbd):
            a = slot[k * bsz : (k + 1) * bsz, :]
            cp = jnp.max(jnp.abs(a), axis=0, keepdims=True)
            hit = (cio == cols[k : k + 1, :]) & (tile[nbd + k : nbd + k + 1, :] >= 0.0)
            colmax = jnp.maximum(colmax, jnp.where(hit, cp, 0.0))
    scale = 1.0 / jnp.sqrt(jnp.maximum(colmax, 0.5))
    dc[...] = scale
    got = backward(nbd, R, C, origins, slots, g1, w_ref, wr, part, cb)
    tau = eta / omega
    grad = scale * cost[...] - got * scale
    xp = x_prev[...]
    xn = jnp.clip(xp - tau * grad, 0.0, upper[...] / scale)
    x_new[...] = xn
    v1 = scale * xn
    v2 = scale * (xn - xp)
    own = slots[0]
    cols = own[own.shape[0] - up(nbd, 8) :, :]
    res = []
    for k in range(nbd):
        a = own[k * bsz : (k + 1) * bsz, :]
        hit = cio == cols[k : k + 1, :]
        for v in (v1, v2):
            vk = jnp.sum(jnp.where(hit, v, 0.0), axis=0, keepdims=True)
            res.append(jnp.sum(a * vk, axis=1, keepdims=True))
    rows = rows_of(res, bsz)[: p3.shape[1]]
    p3[...] = jnp.broadcast_to(rows[None], p3.shape)


def dual_kernel(nbd, R, C, origins, g1, g3, *refs):
    slots = refs[:R]
    aux, x_new, dr, dc, y_new, p4, dual, w_ref, wr, part = refs[R:]
    me_r = lax.axis_index("row")
    cb, bsz = x_new.shape
    x_prev, cost, upper = (aux.at[i * cb : (i + 1) * cb] for i in range(3))
    eta, omega = (aux[3 * cb + i : 3 * cb + i + 1, :] for i in range(2))
    rb = dr.shape[0] // R
    base = nbd * bsz
    rio = iota((rb, bsz), 0).astype(F32)
    wr[...] = jnp.zeros_like(wr)
    sigma = eta * omega
    dr_all = []
    for s, slot in enumerate(slots):
        q = origins(me_r, s)
        at = pl.ds(pl.multiple_of(q * rb, rb), rb)

        def body(c, acc):
            one, two = acc
            tile = g1[q * C + c]
            got = g3[q * C + c]
            for k in range(nbd):
                hit = rio == tile[nbd + k : nbd + k + 1, :]
                one = one + jnp.where(hit, got[2 * k : 2 * k + 1, :], 0.0)
                two = two + jnp.where(hit, got[2 * k + 1 : 2 * k + 2, :], 0.0)
            return one, two

        zero = jnp.zeros((rb, bsz), F32)
        ax, adx = lax.fori_loop(0, C, body, (zero, zero), unroll=min(C, 8))
        scale = dr[at, :]
        ax = ax * scale
        adx = adx * scale
        bs = scale * slot[base + rb : base + 2 * rb, :]
        yp = slot[base : base + rb, :]
        yn = yp + sigma * (bs - ax - adx)
        if s == 0:
            y_new[...] = yn
        w_ref[at, :] = scale * yn
        dy = yn - yp
        resid = bs - ax
        for i, term in enumerate((dy * dy, adx * adx, resid * resid, bs * yn)):
            part[q, i : i + 1, :] = jnp.sum(term, axis=0, keepdims=True)
    sums = part[0, :4, :]
    for q in range(1, R):
        sums += part[q, :4, :]
    dual[:4, :] = jnp.broadcast_to(jnp.sum(sums, axis=1, keepdims=True), (4, bsz))
    dual[4:, :] = jnp.broadcast_to(omega, (4, bsz))
    got = backward(nbd, R, C, origins, slots, g1, w_ref, wr, part, cb)
    scale = dc[...]
    cs = scale * cost[...]
    reduced = cs - got * scale
    us = upper[...] / scale
    xn = x_new[...]
    dx = xn - x_prev[...]
    lane = iota((1, bsz), 1)
    out = jnp.zeros((1, bsz), F32)
    for i, term in enumerate((dx * dx, cs * xn, us * jnp.maximum(-reduced, 0.0))):
        out = jnp.where(lane == i, jnp.sum(term), out)
    p4[...] = jnp.broadcast_to(out, p4.shape)


def stats_kernel(total_rows, total_cols, g4, dual, x_new, y_new, stats, x_out, y_out, sems):
    outs = [
        pltpu.make_async_copy(x_new, x_out, sems.at[0]),
        pltpu.make_async_copy(y_new, y_out, sems.at[1]),
    ]
    for copy in outs:
        copy.start()
    bsz = g4.shape[1]
    primal = jnp.sum(g4[...], axis=0, keepdims=True)
    lane = iota((1, bsz), 1)

    def pick(i):
        return jnp.sum(jnp.where(lane == i, primal, 0.0), axis=1, keepdims=True)

    dx2, cx, uneg = (jnp.broadcast_to(pick(i), (1, bsz)) for i in range(3))
    dy2, adx2, res2, by = (dual[i : i + 1, :] for i in range(4))
    omega = dual[4:5, :]
    movement = 0.5 * omega * dx2 + 0.5 / omega * dy2
    first = jnp.sqrt(res2 / total_rows)
    second = (cx - by + uneg) / total_cols
    third = movement / jnp.sqrt(adx2 * dy2 + 1e-06)
    out = jnp.where(lane == 0, first, jnp.where(lane == 1, second, third))
    stats[...] = out[:, : stats.shape[1]]
    for copy in outs:
        copy.wait()


def shards(blocks, block_rows, block_cols, counts, x_prev, y_prev, cost, rhs, upper, steps):
    R = lax.axis_size("row")
    C = lax.axis_size("col")
    ndev = R * C
    nbd, bsz = blocks.shape[2], blocks.shape[3]
    rb = y_prev.shape[0] // bsz
    cb = x_prev.shape[0] // bsz
    hp = up(2 * nbd, 8)
    y2, rhs2 = y_prev.reshape(rb, bsz), rhs.reshape(rb, bsz)
    x2, cost2, upper2 = (v.reshape(cb, bsz) for v in (x_prev, cost, upper))
    params = pltpu.CompilerParams(vmem_limit_bytes=LIMIT)
    bulk_rows = nbd * bsz + 2 * rb + up(nbd, 8)
    p1, bulk, aux = pl.pallas_call(
        functools.partial(peaks_kernel, nbd),
        out_shape=(
            jax.ShapeDtypeStruct((ndev, hp, bsz), F32),
            jax.ShapeDtypeStruct((bulk_rows, bsz), F32),
            jax.ShapeDtypeStruct((3 * cb + 8, bsz), F32),
        ),
        in_specs=[HBM] * 9 + [SMEM],
        out_specs=(VMEM,) * 3,
        scratch_shapes=[
            pltpu.SMEM((1, 1, nbd), jnp.int32),
            pltpu.SMEM((1, 1, nbd), jnp.int32),
            pltpu.SMEM(steps.shape, F32),
            pltpu.SemaphoreType.DMA((nbd + 8,)),
        ],
        compiler_params=params,
        name="peaks",
    )(
        *(
            pltpu.with_memory_space_constraint(v, pltpu.HBM)
            for v in (blocks[0, 0], y2, rhs2, x2, cost2, upper2, block_rows, block_cols, steps)
        ),
        counts,
    )

    def spread(v):
        return lax.all_to_all(v, ("row", "col"), 0, 0, tiled=True)

    step = R // 2
    ids, slots = [0], [bulk]
    g1 = None
    while step:
        perm = [(i, i ^ step) for i in range(R)]
        slots += [lax.ppermute(b, "row", perm) for b in slots]
        ids += [i ^ step for i in ids]
        if g1 is None:
            g1 = spread(p1)
            g1, *slots[1:] = lax.optimization_barrier((g1, *slots[1:]))
        step //= 2

    def origins(me, s):
        return me ^ ids[s] if ids[s] else me

    scratch = [
        pltpu.VMEM((R * rb, bsz), F32),
        pltpu.VMEM((up(R * nbd, bsz), bsz), F32),
        pltpu.VMEM((R, cb, bsz), F32),
    ]
    x_new, dr, dc, p3 = pl.pallas_call(
        functools.partial(primal_kernel, nbd, R, C, origins),
        out_shape=(
            jax.ShapeDtypeStruct((cb, bsz), F32),
            jax.ShapeDtypeStruct((R * rb, bsz), F32),
            jax.ShapeDtypeStruct((cb, bsz), F32),
            jax.ShapeDtypeStruct((ndev, hp, bsz), F32),
        ),
        in_specs=[VMEM] * (2 + R),
        out_specs=(VMEM,) * 4,
        scratch_shapes=scratch,
        compiler_params=params,
        name="primal",
    )(g1, *slots, aux)
    g3 = spread(p3)
    y_new, p4, dual = pl.pallas_call(
        functools.partial(dual_kernel, nbd, R, C, origins),
        out_shape=(
            jax.ShapeDtypeStruct((rb, bsz), F32),
            jax.ShapeDtypeStruct((C, bsz), F32),
            jax.ShapeDtypeStruct((8, bsz), F32),
        ),
        in_specs=[VMEM] * (2 + R + 4),
        out_specs=(VMEM,) * 3,
        scratch_shapes=scratch,
        compiler_params=params,
        name="dual",
    )(g1, g3, *slots, aux, x_new, dr, dc)
    g4 = lax.all_to_all(p4, "col", 0, 0, tiled=True)
    stats, x_new, y_new = pl.pallas_call(
        functools.partial(
            stats_kernel, float(y_prev.shape[0] * R), float(x_prev.shape[0] * C)
        ),
        out_shape=(
            jax.ShapeDtypeStruct((1, 3), F32),
            jax.ShapeDtypeStruct((cb, bsz), F32),
            jax.ShapeDtypeStruct((rb, bsz), F32),
        ),
        in_specs=[VMEM] * 4,
        out_specs=(VMEM, HBM, HBM),
        scratch_shapes=[pltpu.SemaphoreType.DMA((2,))],
        compiler_params=params,
        name="stats",
    )(g4, dual, x_new, y_new)
    return (x_new.reshape(-1), y_new.reshape(-1), stats.reshape(-1))


def solution(mesh):
    placed = (
        P("row", "col", None, None, None),
        P("row", "col", None),
        P("row", "col", None),
        P("row", "col"),
        P("col"),
        P("row"),
        P("col"),
        P("row"),
        P("col"),
        P(),
    )
    return jax.shard_map(
        shards, mesh=mesh, in_specs=placed, out_specs=(P("col"), P("row"), P()), check_vma=False
    )
```

```python
import functools

import jax
import jax.numpy as jnp
from jax import lax
from jax.experimental import pallas as pl
from jax.experimental.pallas import tpu as pltpu
from jax.sharding import PartitionSpec as P

F32 = jnp.float32
VMEM = pl.BlockSpec(memory_space=pltpu.VMEM)
SMEM = pl.BlockSpec(memory_space=pltpu.SMEM)
HBM = pl.BlockSpec(memory_space=pltpu.HBM)
LIMIT = 40 * 1024 * 1024


def up(n, m):
    return -(-n // m) * m


def iota(shape, dim):
    return lax.broadcasted_iota(jnp.int32, shape, dim)


def rows_of(vectors, bsz):
    lane = iota((bsz, bsz), 1)
    cols = jnp.zeros((bsz, bsz), F32)
    for k, col in enumerate(vectors):
        cols = jnp.where(lane == k, col, cols)
    return cols.T


def total(rows):
    return jnp.sum(rows, axis=0, keepdims=True)


def peaks_kernel(nbd, blocks, y, rhs, x, cost, upper, brow, bcol, steps, count, p1, bulk, aux, *scratch):
    s_row, s_col, s_steps, sems = scratch
    bsz = bulk.shape[1]
    rb = y.shape[0]
    cb = x.shape[0]
    base = nbd * bsz
    pairs = [
        (brow, s_row),
        (bcol, s_col),
        (steps, s_steps),
        (y, bulk.at[base : base + rb]),
        (rhs, bulk.at[base + rb : base + 2 * rb]),
        (x, aux.at[:cb]),
        (cost, aux.at[cb : 2 * cb]),
        (upper, aux.at[2 * cb : 3 * cb]),
    ]
    loads = [
        pltpu.make_async_copy(blocks.at[k], bulk.at[k * bsz : (k + 1) * bsz], sems.at[k])
        for k in range(nbd)
    ]
    rest = [pltpu.make_async_copy(a, b, sems.at[nbd + i]) for i, (a, b) in enumerate(pairs)]
    for copy in loads + rest:
        copy.start()
    peaks = []
    for k in range(nbd):
        loads[k].wait()
        a = bulk[k * bsz : (k + 1) * bsz, :]
        peaks.append(jnp.max(jnp.abs(a), axis=1, keepdims=True))
    rows = rows_of(peaks, bsz)
    for copy in rest:
        copy.wait()
    lane = iota((1, bsz), 1)
    meta = jnp.full((1, bsz), -1.0, F32)
    for k in range(nbd):
        code = jnp.where(k < count[0, 0], s_row[0, 0, k], -1).astype(F32)
        meta = jnp.where(lane == k, code, meta)
        meta = jnp.where(lane == nbd + k, s_col[0, 0, k].astype(F32), meta)
    pieces = [rows[k : k + 1, :] for k in range(nbd)] + [meta]
    for k, piece in enumerate(pieces):
        p1[:, :, k * bsz : (k + 1) * bsz] = jnp.broadcast_to(piece[None], (p1.shape[0], 1, bsz))
    asub = iota((8, bsz), 0)
    aux[3 * cb :, :] = jnp.where(asub == 0, s_steps[0], s_steps[1])


def backward(nbd, rb, cb, q, slot, codes, w_ref, wr):
    me_c = lax.axis_index("col")
    bsz = slot.shape[1]
    rio = iota((rb, bsz), 0).astype(F32)
    cio = iota((cb, bsz), 0).astype(F32)
    w = w_ref[pl.ds(pl.multiple_of(q * rb, rb), rb), :]
    for k in range(nbd):
        hit = rio == codes[q, k, pl.ds(me_c, 1), :]
        wr[k : k + 1, :] = total(jnp.where(hit, w, 0.0))
    wt = wr[...].T
    out = jnp.zeros((cb, bsz), F32)
    for k in range(nbd):
        prod = total(slot[k * bsz : (k + 1) * bsz, :] * wt[:, k : k + 1])
        out += jnp.where(cio == codes[q, nbd + k, pl.ds(me_c, 1), :], prod, 0.0)
    return out


def col_peaks(nbd, cb, q, slot, codes):
    me_c = lax.axis_index("col")
    bsz = slot.shape[1]
    cio = iota((cb, bsz), 0).astype(F32)
    out = jnp.zeros((cb, bsz), F32)
    for k in range(nbd):
        peak = jnp.max(jnp.abs(slot[k * bsz : (k + 1) * bsz, :]), axis=0, keepdims=True)
        live = codes[q, k, pl.ds(me_c, 1), :] >= 0.0
        hit = (cio == codes[q, nbd + k, pl.ds(me_c, 1), :]) & live
        out = jnp.maximum(out, jnp.where(hit, peak, 0.0))
    return out


def scales_kernel(nbd, R, C, rb, cb, origins, g1, *refs):
    half = max(R // 2, 1)
    slots = refs[:half]
    dr, codes, part, colmax, w_ref, wr = refs[half:]
    me_r = lax.axis_index("row")
    bsz = dr.shape[1]
    base = nbd * bsz
    rio = iota((rb, bsz), 0).astype(F32)
    wr[...] = jnp.zeros_like(wr)
    for q in range(R):
        meta = g1[q * C : (q + 1) * C, 0, base:]
        for k in range(2 * nbd):
            codes[q, k] = jnp.broadcast_to(meta[:, k : k + 1], (C, bsz))

        def body(c, acc):
            for k in range(nbd):
                hit = rio == codes[q, k, pl.ds(c, 1), :]
                acc = jnp.maximum(acc, jnp.where(hit, g1[q * C + c, :, k * bsz : (k + 1) * bsz], 0.0))
            return acc

        peak = lax.fori_loop(0, C, body, jnp.zeros((rb, bsz), F32), unroll=min(C, 8))
        dr[q * rb : (q + 1) * rb, :] = 1.0 / jnp.sqrt(jnp.maximum(peak, 0.5))
    top = jnp.zeros((cb, bsz), F32)
    for s, slot in enumerate(slots):
        q = origins(me_r, s)
        at = pl.ds(pl.multiple_of(q * rb, rb), rb)
        w_ref[at, :] = dr[at, :] * slot[base : base + rb, :]
        top = jnp.maximum(top, col_peaks(nbd, cb, q, slot, codes))
        part[q] = backward(nbd, rb, cb, q, slot, codes, w_ref, wr)
    colmax[...] = top


def primal_kernel(nbd, R, C, rb, cb, origins, *refs):
    half = max(R // 2, 1)
    slots, own = refs[: R - half], refs[R - half]
    aux, dr, codes, done, colmax, x_new, dc, p3, w_ref, wr, part = refs[R - half + 1 :]
    me_r = lax.axis_index("row")
    me_c = lax.axis_index("col")
    bsz = x_new.shape[1]
    base = nbd * bsz
    x_prev, cost, upper = (aux[i * cb : (i + 1) * cb, :] for i in range(3))
    eta, omega = (aux[3 * cb + i : 3 * cb + i + 1, :] for i in range(2))
    cio = iota((cb, bsz), 0).astype(F32)
    wr[...] = jnp.zeros_like(wr)
    top = colmax[...]
    for s in range(half):
        q = origins(me_r, s)
        part[q] = done[q]
    for s, slot in enumerate(slots):
        q = origins(me_r, half + s)
        at = pl.ds(pl.multiple_of(q * rb, rb), rb)
        w_ref[at, :] = dr[at, :] * slot[base : base + rb, :]
        top = jnp.maximum(top, col_peaks(nbd, cb, q, slot, codes))
        part[q] = backward(nbd, rb, cb, q, slot, codes, w_ref, wr)
    got = part[0]
    for q in range(1, R):
        got += part[q]
    scale = 1.0 / jnp.sqrt(jnp.maximum(top, 0.5))
    dc[...] = scale
    grad = scale * cost - got * scale
    xn = jnp.clip(x_prev - eta / omega * grad, 0.0, upper / scale)
    x_new[...] = xn
    v1 = scale * xn
    v2 = scale * (xn - x_prev)
    res = []
    for k in range(nbd):
        a = own[k * bsz : (k + 1) * bsz, :]
        hit = cio == codes[me_r, nbd + k, pl.ds(me_c, 1), :]
        for v in (v1, v2):
            res.append(jnp.sum(a * total(jnp.where(hit, v, 0.0)), axis=1, keepdims=True))
    rows = rows_of(res, bsz)[: p3.shape[1]]
    p3[...] = jnp.broadcast_to(rows[None], p3.shape)


def dual_kernel(nbd, R, C, rb, cb, origins, g3, *refs):
    slots = refs[:R]
    aux, dr, codes, x_new, dc, y_new, p4, dual, w_ref, wr, part = refs[R:]
    me_r = lax.axis_index("row")
    bsz = x_new.shape[1]
    base = nbd * bsz
    x_prev, cost, upper = (aux[i * cb : (i + 1) * cb, :] for i in range(3))
    eta, omega = (aux[3 * cb + i : 3 * cb + i + 1, :] for i in range(2))
    rio = iota((rb, bsz), 0).astype(F32)
    wr[...] = jnp.zeros_like(wr)
    sigma = eta * omega
    for s, slot in enumerate(slots):
        q = origins(me_r, s)
        at = pl.ds(pl.multiple_of(q * rb, rb), rb)

        def body(c, acc):
            one, two = acc
            got = g3[q * C + c]
            for k in range(nbd):
                hit = rio == codes[q, k, pl.ds(c, 1), :]
                one = one + jnp.where(hit, got[2 * k : 2 * k + 1, :], 0.0)
                two = two + jnp.where(hit, got[2 * k + 1 : 2 * k + 2, :], 0.0)
            return one, two

        zero = jnp.zeros((rb, bsz), F32)
        ax, adx = lax.fori_loop(0, C, body, (zero, zero), unroll=min(C, 8))
        scale = dr[at, :]
        ax = ax * scale
        adx = adx * scale
        bs = scale * slot[base + rb : base + 2 * rb, :]
        yp = slot[base : base + rb, :]
        yn = yp + sigma * (bs - ax - adx)
        if s == 0:
            y_new[...] = yn
        w_ref[at, :] = scale * yn
        dy = yn - yp
        resid = bs - ax
        for i, term in enumerate((dy * dy, adx * adx, resid * resid, bs * yn)):
            part[q, i : i + 1, :] = total(term)
    sums = part[0, :4, :]
    for q in range(1, R):
        sums += part[q, :4, :]
    dual[:4, :] = jnp.broadcast_to(jnp.sum(sums, axis=1, keepdims=True), (4, bsz))
    dual[4:, :] = jnp.broadcast_to(omega, (4, bsz))
    for s, slot in enumerate(slots):
        q = origins(me_r, s)
        part[q] = backward(nbd, rb, cb, q, slot, codes, w_ref, wr)
    got = part[0]
    for q in range(1, R):
        got += part[q]
    scale = dc[...]
    cs = scale * cost
    reduced = cs - got * scale
    us = upper / scale
    xn = x_new[...]
    dx = xn - x_prev
    lane = iota((1, bsz), 1)
    out = jnp.zeros((1, bsz), F32)
    for i, term in enumerate((dx * dx, cs * xn, us * jnp.maximum(-reduced, 0.0))):
        out = jnp.where(lane == i, jnp.sum(term), out)
    p4[...] = jnp.broadcast_to(out[None], p4.shape)


def stats_kernel(C, total_rows, total_cols, g4, dual, x_new, y_new, stats, x_out, y_out, sems):
    outs = [
        pltpu.make_async_copy(x_new, x_out, sems.at[0]),
        pltpu.make_async_copy(y_new, y_out, sems.at[1]),
    ]
    for copy in outs:
        copy.start()
    bsz = g4.shape[2]
    primal = g4[0]
    for c in range(1, C):
        primal += g4[c]
    lane = iota((1, bsz), 1)

    def pick(i):
        return jnp.sum(jnp.where(lane == i, primal, 0.0), axis=1, keepdims=True)

    dx2, cx, uneg = (jnp.broadcast_to(pick(i), (1, bsz)) for i in range(3))
    dy2, adx2, res2, by = (dual[i : i + 1, :] for i in range(4))
    omega = dual[4:5, :]
    movement = 0.5 * omega * dx2 + 0.5 / omega * dy2
    first = jnp.sqrt(res2 / total_rows)
    second = (cx - by + uneg) / total_cols
    third = movement / jnp.sqrt(adx2 * dy2 + 1e-06)
    out = jnp.where(lane == 0, first, jnp.where(lane == 1, second, third))
    stats[...] = out[:, : stats.shape[1]]
    for copy in outs:
        copy.wait()


def shards(blocks, block_rows, block_cols, counts, x_prev, y_prev, cost, rhs, upper, steps):
    R = lax.axis_size("row")
    C = lax.axis_size("col")
    ndev = R * C
    nbd, bsz = blocks.shape[2], blocks.shape[3]
    rb = y_prev.shape[0] // bsz
    cb = x_prev.shape[0] // bsz
    half = max(R // 2, 1)
    shape = lambda *dims: jax.ShapeDtypeStruct(dims, F32)
    params = pltpu.CompilerParams(vmem_limit_bytes=LIMIT)
    raw = (
        blocks[0, 0],
        y_prev.reshape(rb, bsz),
        rhs.reshape(rb, bsz),
        x_prev.reshape(cb, bsz),
        cost.reshape(cb, bsz),
        upper.reshape(cb, bsz),
        block_rows,
        block_cols,
        steps,
    )
    p1, bulk, aux = pl.pallas_call(
        functools.partial(peaks_kernel, nbd),
        out_shape=(
            shape(ndev, 1, (nbd + 1) * bsz),
            shape(nbd * bsz + 2 * rb, bsz),
            shape(3 * cb + 8, bsz),
        ),
        in_specs=[HBM] * len(raw) + [SMEM],
        out_specs=(VMEM,) * 3,
        scratch_shapes=[
            pltpu.SMEM((1, 1, nbd), jnp.int32),
            pltpu.SMEM((1, 1, nbd), jnp.int32),
            pltpu.SMEM(steps.shape, F32),
            pltpu.SemaphoreType.DMA((nbd + 8,)),
        ],
        compiler_params=params,
        name="peaks",
    )(*(pltpu.with_memory_space_constraint(v, pltpu.HBM) for v in raw), counts)

    def spread(v):
        return lax.all_to_all(v, ("row", "col"), 0, 0, tiled=True)

    step = R // 2
    ids, slots = [0], [bulk]
    while step > 1:
        slots += [lax.ppermute(b, "row", [(i, i ^ step) for i in range(R)]) for b in slots]
        ids += [i ^ step for i in ids]
        step //= 2
    g1 = spread(p1)
    g1, bulk, *slots = lax.optimization_barrier((g1, bulk, *slots[1:]))
    slots = [bulk, *slots]
    if R > 1:
        slots += [lax.ppermute(b, "row", [(i, i ^ 1) for i in range(R)]) for b in slots]
        ids += [i ^ 1 for i in ids]

    def origins(me, s):
        return me ^ ids[s] if ids[s] else me

    scratch = [
        pltpu.VMEM((R * rb, bsz), F32),
        pltpu.VMEM((up(nbd, bsz), bsz), F32),
    ]
    part = pltpu.VMEM((R, up(cb, 8), bsz), F32)
    sizes = (nbd, R, C, rb, cb, origins)
    dr, codes, done, colmax = pl.pallas_call(
        functools.partial(scales_kernel, *sizes),
        out_shape=(
            shape(R * rb, bsz),
            shape(R, 2 * nbd, C, bsz),
            shape(R, cb, bsz),
            shape(cb, bsz),
        ),
        in_specs=[VMEM] * (1 + half),
        out_specs=(VMEM,) * 4,
        scratch_shapes=scratch,
        compiler_params=params,
        name="scales",
    )(g1, *slots[:half])
    x_new, dc, p3 = pl.pallas_call(
        functools.partial(primal_kernel, *sizes),
        out_shape=(shape(cb, bsz), shape(cb, bsz), shape(ndev, up(2 * nbd, 8), bsz)),
        in_specs=[VMEM] * (R - half + 6),
        out_specs=(VMEM,) * 3,
        scratch_shapes=scratch + [part],
        compiler_params=params,
        name="primal",
    )(*slots[half:], bulk, aux, dr, codes, done, colmax)
    g3 = spread(p3)
    y_new, p4, dual = pl.pallas_call(
        functools.partial(dual_kernel, *sizes),
        out_shape=(shape(rb, bsz), shape(ndev, 1, bsz), shape(8, bsz)),
        in_specs=[VMEM] * (R + 6),
        out_specs=(VMEM,) * 3,
        scratch_shapes=scratch + [part],
        compiler_params=params,
        name="dual",
    )(g3, *slots, aux, dr, codes, x_new, dc)
    g4 = spread(p4)
    stats, x_new, y_new = pl.pallas_call(
        functools.partial(
            stats_kernel, C, float(y_prev.shape[0] * R), float(x_prev.shape[0] * C)
        ),
        out_shape=(shape(1, 3), shape(cb, bsz), shape(rb, bsz)),
        in_specs=[VMEM] * 4,
        out_specs=(VMEM, HBM, HBM),
        scratch_shapes=[pltpu.SemaphoreType.DMA((2,))],
        compiler_params=params,
        name="stats",
    )(g4, dual, x_new, y_new)
    return (x_new.reshape(-1), y_new.reshape(-1), stats.reshape(-1))


def solution(mesh):
    placed = (
        P("row", "col", None, None, None),
        P("row", "col", None),
        P("row", "col", None),
        P("row", "col"),
        P("col"),
        P("row"),
        P("col"),
        P("row"),
        P("col"),
        P(),
    )
    return jax.shard_map(
        shards, mesh=mesh, in_specs=placed, out_specs=(P("col"), P("row"), P()), check_vma=False
    )
```

```python
import functools

import jax
import jax.numpy as jnp
from jax import lax
from jax.experimental import pallas as pl
from jax.experimental.pallas import tpu as pltpu
from jax.sharding import PartitionSpec as P

F32 = jnp.float32
VMEM = pl.BlockSpec(memory_space=pltpu.VMEM)
SMEM = pl.BlockSpec(memory_space=pltpu.SMEM)
HBM = pl.BlockSpec(memory_space=pltpu.HBM)
LIMIT = 40 * 1024 * 1024


def up(n, m):
    return -(-n // m) * m


def iota(shape, dim):
    return lax.broadcasted_iota(jnp.int32, shape, dim)


def rows_of(vectors, bsz):
    lane = iota((bsz, bsz), 1)
    cols = jnp.zeros((bsz, bsz), F32)
    for k, col in enumerate(vectors):
        cols = jnp.where(lane == k, col, cols)
    return cols.T


def total(rows):
    return jnp.sum(rows, axis=0, keepdims=True)


def peaks_kernel(nbd, blocks, y, rhs, x, cost, upper, brow, bcol, steps, count, p1, bulk, aux, *scratch):
    s_row, s_col, s_steps, sems = scratch
    bsz = bulk.shape[1]
    rb = y.shape[0]
    cb = x.shape[0]
    base = nbd * bsz
    pairs = [
        (brow, s_row),
        (bcol, s_col),
        (steps, s_steps),
        (y, bulk.at[base : base + rb]),
        (rhs, bulk.at[base + rb : base + 2 * rb]),
        (x, aux.at[:cb]),
        (cost, aux.at[cb : 2 * cb]),
        (upper, aux.at[2 * cb : 3 * cb]),
    ]
    loads = [
        pltpu.make_async_copy(blocks.at[k], bulk.at[k * bsz : (k + 1) * bsz], sems.at[k])
        for k in range(nbd)
    ]
    rest = [pltpu.make_async_copy(a, b, sems.at[nbd + i]) for i, (a, b) in enumerate(pairs)]
    for copy in loads + rest:
        copy.start()
    peaks = []
    for k in range(nbd):
        loads[k].wait()
        a = bulk[k * bsz : (k + 1) * bsz, :]
        peaks.append(jnp.max(jnp.abs(a), axis=1, keepdims=True))
    rows = rows_of(peaks, bsz)
    for copy in rest:
        copy.wait()
    lane = iota((1, bsz), 1)
    meta = jnp.full((1, bsz), -1.0, F32)
    for k in range(nbd):
        code = jnp.where(k < count[0, 0], s_row[0, 0, k], -1).astype(F32)
        meta = jnp.where(lane == k, code, meta)
        meta = jnp.where(lane == nbd + k, s_col[0, 0, k].astype(F32), meta)
    pieces = [rows[k : k + 1, :] for k in range(nbd)] + [meta]
    for k, piece in enumerate(pieces):
        p1[:, :, k * bsz : (k + 1) * bsz] = jnp.broadcast_to(piece[None], (p1.shape[0], 1, bsz))
    asub = iota((8, bsz), 0)
    aux[3 * cb :, :] = jnp.where(asub == 0, s_steps[0], s_steps[1])


def backward(nbd, rb, cb, q, slot, codes, w_ref, wr):
    me_c = lax.axis_index("col")
    bsz = slot.shape[1]
    rio = iota((rb, bsz), 0).astype(F32)
    cio = iota((cb, bsz), 0).astype(F32)
    w = w_ref[pl.ds(pl.multiple_of(q * rb, rb), rb), :]
    for k in range(nbd):
        hit = rio == codes[q, k, pl.ds(me_c, 1), :]
        wr[k : k + 1, :] = total(jnp.where(hit, w, 0.0))
    wt = wr[...].T
    out = jnp.zeros((cb, bsz), F32)
    for k in range(nbd):
        prod = total(slot[k * bsz : (k + 1) * bsz, :] * wt[:, k : k + 1])
        out += jnp.where(cio == codes[q, nbd + k, pl.ds(me_c, 1), :], prod, 0.0)
    return out


def col_peaks(nbd, cb, q, slot, codes):
    me_c = lax.axis_index("col")
    bsz = slot.shape[1]
    cio = iota((cb, bsz), 0).astype(F32)
    out = jnp.zeros((cb, bsz), F32)
    for k in range(nbd):
        peak = jnp.max(jnp.abs(slot[k * bsz : (k + 1) * bsz, :]), axis=0, keepdims=True)
        live = codes[q, k, pl.ds(me_c, 1), :] >= 0.0
        hit = (cio == codes[q, nbd + k, pl.ds(me_c, 1), :]) & live
        out = jnp.maximum(out, jnp.where(hit, peak, 0.0))
    return out


def scales_kernel(nbd, R, C, rb, cb, origins, g1, *refs):
    half = min(R, 2)
    slots = refs[:half]
    dr, codes, packed, part, colmax, w_ref, wr = refs[half:]
    me_r = lax.axis_index("row")
    bsz = dr.shape[1]
    base = nbd * bsz
    rio = iota((rb, bsz), 0).astype(F32)
    wr[...] = jnp.zeros_like(wr)
    for q in range(R):
        meta = g1[q * C : (q + 1) * C, 0, base:]
        for k in range(2 * nbd):
            codes[q, k] = jnp.broadcast_to(meta[:, k : k + 1], (C, bsz))

        def body(c, acc):
            for k in range(nbd):
                hit = rio == codes[q, k, pl.ds(c, 1), :]
                acc = jnp.maximum(acc, jnp.where(hit, g1[q * C + c, :, k * bsz : (k + 1) * bsz], 0.0))
            return acc

        peak = lax.fori_loop(0, C, body, jnp.zeros((rb, bsz), F32), unroll=min(C, 8))
        dr[q * rb : (q + 1) * rb, :] = 1.0 / jnp.sqrt(jnp.maximum(peak, 0.5))
    share = iota((C, bsz), 1) // (bsz // C)
    mine = jnp.full((C, bsz), -1.0, F32)
    for k in range(nbd):
        mine = jnp.where(share == k, codes[me_r, k], mine)
    packed[...] = mine
    top = jnp.zeros((cb, bsz), F32)
    for s, slot in enumerate(slots):
        q = origins(me_r, s)
        at = pl.ds(pl.multiple_of(q * rb, rb), rb)
        w_ref[at, :] = dr[at, :] * slot[base : base + rb, :]
        top = jnp.maximum(top, col_peaks(nbd, cb, q, slot, codes))
        part[q] = backward(nbd, rb, cb, q, slot, codes, w_ref, wr)
    colmax[...] = top


def primal_kernel(nbd, R, C, rb, cb, origins, *refs):
    half = min(R, 2)
    slots, own = refs[: R - half], refs[R - half]
    aux, dr, codes, done, colmax, x_new, dc, p3, w_ref, wr, part = refs[R - half + 1 :]
    me_r = lax.axis_index("row")
    me_c = lax.axis_index("col")
    bsz = x_new.shape[1]
    base = nbd * bsz
    x_prev, cost, upper = (aux[i * cb : (i + 1) * cb, :] for i in range(3))
    eta, omega = (aux[3 * cb + i : 3 * cb + i + 1, :] for i in range(2))
    cio = iota((cb, bsz), 0).astype(F32)
    wr[...] = jnp.zeros_like(wr)
    top = colmax[...]
    for s in range(half):
        q = origins(me_r, s)
        part[q] = done[q]
    for s, slot in enumerate(slots):
        q = origins(me_r, half + s)
        at = pl.ds(pl.multiple_of(q * rb, rb), rb)
        w_ref[at, :] = dr[at, :] * slot[base : base + rb, :]
        top = jnp.maximum(top, col_peaks(nbd, cb, q, slot, codes))
        part[q] = backward(nbd, rb, cb, q, slot, codes, w_ref, wr)
    got = part[0]
    for q in range(1, R):
        got += part[q]
    scale = 1.0 / jnp.sqrt(jnp.maximum(top, 0.5))
    dc[...] = scale
    grad = scale * cost - got * scale
    xn = jnp.clip(x_prev - eta / omega * grad, 0.0, upper / scale)
    x_new[...] = xn
    v2 = scale * (xn - x_prev)
    v1 = scale * xn + v2
    both, step = [], []
    for k in range(nbd):
        a = own[k * bsz : (k + 1) * bsz, :]
        hit = cio == codes[me_r, nbd + k, pl.ds(me_c, 1), :]
        for v, out in ((v1, both), (v2, step)):
            out.append(jnp.sum(a * total(jnp.where(hit, v, 0.0)), axis=1, keepdims=True))
    rows = rows_of(both + step, bsz)
    lanes = bsz // C
    share = iota((C, bsz), 1) // lanes
    row = jnp.zeros((C, bsz), F32)
    for k in range(nbd):
        part_k = pltpu.roll(rows[nbd + k : nbd + k + 1, :], (k + 1) * lanes % bsz, 1)
        part_k = jnp.broadcast_to(part_k, (C, bsz))
        part_k = pltpu.roll(part_k, 0, 1, stride=lanes, stride_axis=0)
        row = jnp.where(share == k, part_k, row)
        p3[:, :, k * bsz : (k + 1) * bsz] = jnp.broadcast_to(
            rows[k : k + 1, :][None], (p3.shape[0], 1, bsz)
        )
    for q in range(R):
        p3[q * C : (q + 1) * C, 0, base:] = row


def dual_kernel(nbd, R, C, rb, cb, origins, g3, *refs):
    slots = refs[:R]
    aux, dr, codes, packed, x_new, dc, y_new, p4, dual, w_ref, wr, part = refs[R:]
    me_r = lax.axis_index("row")
    me_c = lax.axis_index("col")
    bsz = x_new.shape[1]
    base = nbd * bsz
    x_prev, cost, upper = (aux[i * cb : (i + 1) * cb, :] for i in range(3))
    eta, omega = (aux[3 * cb + i : 3 * cb + i + 1, :] for i in range(2))
    rio = iota((rb, bsz), 0).astype(F32)
    wr[...] = jnp.zeros_like(wr)
    sigma = eta * omega
    for s, slot in enumerate(slots):
        q = origins(me_r, s)
        at = pl.ds(pl.multiple_of(q * rb, rb), rb)

        def body(c, acc):
            for k in range(nbd):
                hit = rio == codes[q, k, pl.ds(c, 1), :]
                acc = acc + jnp.where(hit, g3[q * C + c, :, k * bsz : (k + 1) * bsz], 0.0)
            return acc

        both = lax.fori_loop(0, C, body, jnp.zeros((rb, bsz), F32), unroll=min(C, 8))
        scale = dr[at, :]
        both = both * scale
        bs = scale * slot[base + rb : base + 2 * rb, :]
        yp = slot[base : base + rb, :]
        yn = yp + sigma * (bs - both)
        w_ref[at, :] = scale * yn
        dy = yn - yp
        part[q, 0:1, :] = total(dy * dy)
        part[q, 1:2, :] = total(bs * yn)
        if s == 0:
            y_new[...] = yn

            def mine(c, acc):
                hit = rio == packed[pl.ds(c, 1), :]
                return acc + jnp.where(hit, g3[q * C + c, :, base:], 0.0)

            shares = lax.fori_loop(0, C, mine, jnp.zeros((rb, bsz), F32), unroll=min(C, 8))
            lanes = bsz // C
            adx = shares
            for k in range(1, nbd):
                adx = adx + pltpu.roll(shares, bsz - k * lanes, 1)
            adx = pltpu.roll(adx, (C - 1 - me_c) * lanes, 1) * scale
            inside = iota((rb, bsz), 1) // lanes == C - 1 - me_c
            adx = jnp.where(inside, adx, 0.0)
            resid = jnp.where(inside, bs - (both - adx), 0.0)
            adx2 = total(adx * adx)
            res2 = total(resid * resid)
    sums = part[0, :2, :]
    for q in range(1, R):
        sums += part[q, :2, :]
    dual[:2, :] = jnp.broadcast_to(jnp.sum(sums, axis=1, keepdims=True), (2, bsz))
    dual[2:, :] = jnp.broadcast_to(omega, (6, bsz))
    for s, slot in enumerate(slots):
        q = origins(me_r, s)
        part[q] = backward(nbd, rb, cb, q, slot, codes, w_ref, wr)
    got = part[0]
    for q in range(1, R):
        got += part[q]
    scale = dc[...]
    cs = scale * cost
    reduced = cs - got * scale
    us = upper / scale
    xn = x_new[...]
    dx = xn - x_prev
    terms = [total(dx * dx), total(cs * xn), total(us * jnp.maximum(-reduced, 0.0)), adx2, res2]
    sub, lane = iota((8, bsz), 0), iota((8, bsz), 1)
    stack = jnp.zeros((8, bsz), F32)
    for i, term in enumerate(terms):
        stack = jnp.where(sub == i, term, stack)
    sums = jnp.sum(stack, axis=1, keepdims=True)
    out = total(jnp.where(sub == lane, sums, 0.0))
    p4[...] = jnp.broadcast_to(out[None], p4.shape)


def stats_kernel(C, total_rows, total_cols, g4, dual, x_new, y_new, stats, x_out, y_out, sems):
    outs = [
        pltpu.make_async_copy(x_new, x_out, sems.at[0]),
        pltpu.make_async_copy(y_new, y_out, sems.at[1]),
    ]
    for copy in outs:
        copy.start()
    bsz = g4.shape[2]
    sums = g4[0]
    for c in range(1, C):
        sums += g4[c]
    every = sums
    for d in range(C, g4.shape[0]):
        every += g4[d]
    sub, lane = iota((8, bsz), 0), iota((8, bsz), 1)
    stack = jnp.where(lane < 3, sums, every)
    stack = jnp.broadcast_to(
        jnp.sum(jnp.where(sub == lane, stack, 0.0), axis=1, keepdims=True), (8, bsz)
    )
    dx2, cx, uneg, adx2, res2 = (stack[i : i + 1, :] for i in range(5))
    dy2, by = (dual[i : i + 1, :] for i in range(2))
    lane = lane[:1]
    omega = dual[2:3, :]
    movement = 0.5 * omega * dx2 + 0.5 / omega * dy2
    first = jnp.sqrt(res2 / total_rows)
    second = (cx - by + uneg) / total_cols
    third = movement / jnp.sqrt(adx2 * dy2 + 1e-06)
    out = jnp.where(lane == 0, first, jnp.where(lane == 1, second, third))
    stats[...] = out[:, : stats.shape[1]]
    for copy in outs:
        copy.wait()


def shards(blocks, block_rows, block_cols, counts, x_prev, y_prev, cost, rhs, upper, steps):
    R = lax.axis_size("row")
    C = lax.axis_size("col")
    ndev = R * C
    nbd, bsz = blocks.shape[2], blocks.shape[3]
    rb = y_prev.shape[0] // bsz
    cb = x_prev.shape[0] // bsz
    half = min(R, 2)
    shape = lambda *dims: jax.ShapeDtypeStruct(dims, F32)
    params = pltpu.CompilerParams(vmem_limit_bytes=LIMIT)
    raw = (
        blocks[0, 0],
        y_prev.reshape(rb, bsz),
        rhs.reshape(rb, bsz),
        x_prev.reshape(cb, bsz),
        cost.reshape(cb, bsz),
        upper.reshape(cb, bsz),
        block_rows,
        block_cols,
        steps,
    )
    p1, bulk, aux = pl.pallas_call(
        functools.partial(peaks_kernel, nbd),
        out_shape=(
            shape(ndev, 1, (nbd + 1) * bsz),
            shape(nbd * bsz + 2 * rb, bsz),
            shape(3 * cb + 8, bsz),
        ),
        in_specs=[HBM] * len(raw) + [SMEM],
        out_specs=(VMEM,) * 3,
        scratch_shapes=[
            pltpu.SMEM((1, 1, nbd), jnp.int32),
            pltpu.SMEM((1, 1, nbd), jnp.int32),
            pltpu.SMEM(steps.shape, F32),
            pltpu.SemaphoreType.DMA((nbd + 8,)),
        ],
        compiler_params=params,
        name="peaks",
    )(*(pltpu.with_memory_space_constraint(v, pltpu.HBM) for v in raw), counts)

    def spread(v):
        return lax.all_to_all(v, ("row", "col"), 0, 0, tiled=True)

    def swap(v, step):
        return lax.ppermute(v, "row", [(i, i ^ step) for i in range(R)])

    far, far_ids, step = [bulk], [0], R // 2
    while step > 1:
        far += [swap(v, step) for v in far]
        far_ids += [i ^ step for i in far_ids]
        step //= 2
    slots, ids = far[:1], [0]
    if R > 1:
        slots.append(swap(bulk, 1))
        ids.append(1)
    g1 = spread(p1)
    g1, slots[-1], *far = lax.optimization_barrier((g1, slots[-1], *far[1:]))
    slots += far + [swap(v, 1) for v in far]
    ids += far_ids[1:] + [i ^ 1 for i in far_ids[1:]]

    def origins(me, s):
        return me ^ ids[s] if ids[s] else me

    scratch = [
        pltpu.VMEM((R * rb, bsz), F32),
        pltpu.VMEM((up(nbd, bsz), bsz), F32),
    ]
    part = pltpu.VMEM((R, up(cb, 8), bsz), F32)
    sizes = (nbd, R, C, rb, cb, origins)
    dr, codes, packed, done, colmax = pl.pallas_call(
        functools.partial(scales_kernel, *sizes),
        out_shape=(
            shape(R * rb, bsz),
            shape(R, 2 * nbd, C, bsz),
            shape(C, bsz),
            shape(R, cb, bsz),
            shape(cb, bsz),
        ),
        in_specs=[VMEM] * (1 + half),
        out_specs=(VMEM,) * 5,
        scratch_shapes=scratch,
        compiler_params=params,
        name="scales",
    )(g1, *slots[:half])
    x_new, dc, p3 = pl.pallas_call(
        functools.partial(primal_kernel, *sizes),
        out_shape=(shape(cb, bsz), shape(cb, bsz), shape(ndev, 1, (nbd + 1) * bsz)),
        in_specs=[VMEM] * (R - half + 6),
        out_specs=(VMEM,) * 3,
        scratch_shapes=scratch + [part],
        compiler_params=params,
        name="primal",
    )(*slots[half:], bulk, aux, dr, codes, done, colmax)
    g3 = spread(p3)
    y_new, p4, dual = pl.pallas_call(
        functools.partial(dual_kernel, *sizes),
        out_shape=(shape(rb, bsz), shape(ndev, 1, bsz), shape(8, bsz)),
        in_specs=[VMEM] * (R + 7),
        out_specs=(VMEM,) * 3,
        scratch_shapes=scratch + [part],
        compiler_params=params,
        name="dual",
    )(g3, *slots, aux, dr, codes, packed, x_new, dc)
    g4 = spread(p4)
    stats, x_new, y_new = pl.pallas_call(
        functools.partial(
            stats_kernel, C, float(y_prev.shape[0] * R), float(x_prev.shape[0] * C)
        ),
        out_shape=(shape(1, 3), shape(cb, bsz), shape(rb, bsz)),
        in_specs=[VMEM] * 4,
        out_specs=(VMEM, HBM, HBM),
        scratch_shapes=[pltpu.SemaphoreType.DMA((2,))],
        compiler_params=params,
        name="stats",
    )(g4, dual, x_new, y_new)
    return (x_new.reshape(-1), y_new.reshape(-1), stats.reshape(-1))


def solution(mesh):
    placed = (
        P("row", "col", None, None, None),
        P("row", "col", None),
        P("row", "col", None),
        P("row", "col"),
        P("col"),
        P("row"),
        P("col"),
        P("row"),
        P("col"),
        P(),
    )
    return jax.shard_map(
        shards, mesh=mesh, in_specs=placed, out_specs=(P("col"), P("row"), P()), check_vma=False
    )
```

```python
import functools

import jax
import jax.numpy as jnp
from jax import lax
from jax.experimental import pallas as pl
from jax.experimental.pallas import tpu as pltpu
from jax.sharding import PartitionSpec as P

F32 = jnp.float32
VMEM = pl.BlockSpec(memory_space=pltpu.VMEM)
SMEM = pl.BlockSpec(memory_space=pltpu.SMEM)
HBM = pl.BlockSpec(memory_space=pltpu.HBM)
LIMIT = 40 * 1024 * 1024


def up(n, m):
    return -(-n // m) * m


def iota(shape, dim):
    return lax.broadcasted_iota(jnp.int32, shape, dim)


def rows_of(vectors, bsz):
    lane = iota((bsz, bsz), 1)
    cols = jnp.zeros((bsz, bsz), F32)
    for k, col in enumerate(vectors):
        cols = jnp.where(lane == k, col, cols)
    return cols.T


def total(rows):
    return jnp.sum(rows, axis=0, keepdims=True)


def peaks_kernel(nbd, blocks, y, rhs, x, cost, upper, brow, bcol, steps, count, p1, bulk, aux, *scratch):
    s_row, s_col, s_steps, sems = scratch
    bsz = bulk.shape[1]
    rb = y.shape[0]
    cb = x.shape[0]
    base = nbd * bsz
    pairs = [
        (brow, s_row),
        (bcol, s_col),
        (steps, s_steps),
        (y, bulk.at[base : base + rb]),
        (rhs, bulk.at[base + rb : base + 2 * rb]),
        (x, aux.at[:cb]),
        (cost, aux.at[cb : 2 * cb]),
        (upper, aux.at[2 * cb : 3 * cb]),
    ]
    loads = [
        pltpu.make_async_copy(blocks.at[k], bulk.at[k * bsz : (k + 1) * bsz], sems.at[k])
        for k in range(nbd)
    ]
    rest = [pltpu.make_async_copy(a, b, sems.at[nbd + i]) for i, (a, b) in enumerate(pairs)]
    for copy in loads + rest:
        copy.start()
    peaks = []
    for k in range(nbd):
        loads[k].wait()
        a = bulk[k * bsz : (k + 1) * bsz, :]
        peaks.append(jnp.max(jnp.abs(a), axis=1, keepdims=True))
    rows = rows_of(peaks, bsz)
    for copy in rest:
        copy.wait()
    lane = iota((1, bsz), 1)
    meta = jnp.full((1, bsz), -1.0, F32)
    for k in range(nbd):
        code = jnp.where(k < count[0, 0], s_row[0, 0, k], -1).astype(F32)
        meta = jnp.where(lane == k, code, meta)
        meta = jnp.where(lane == nbd + k, s_col[0, 0, k].astype(F32), meta)
    pieces = [rows[k : k + 1, :] for k in range(nbd)] + [meta]
    for k, piece in enumerate(pieces):
        p1[:, :, k * bsz : (k + 1) * bsz] = jnp.broadcast_to(piece[None], (p1.shape[0], 1, bsz))
    asub = iota((8, bsz), 0)
    aux[3 * cb :, :] = jnp.where(asub == 0, s_steps[0], s_steps[1])


def weights(nbd, rb, groups, codes, w_ref, wr):
    me_c = lax.axis_index("col")
    bsz = wr.shape[1]
    rio = iota((rb, bsz), 0).astype(F32)
    for s, q in enumerate(groups):
        w = w_ref[pl.ds(pl.multiple_of(q * rb, rb), rb), :]
        for k in range(nbd):
            hit = rio == codes[q, k, pl.ds(me_c, 1), :]
            wr[s * nbd + k : s * nbd + k + 1, :] = total(jnp.where(hit, w, 0.0))
    return wr[...].T


def backward(nbd, cb, q, slot, codes, wt):
    me_c = lax.axis_index("col")
    bsz = slot.shape[1]
    cio = iota((cb, bsz), 0).astype(F32)
    out = jnp.zeros((cb, bsz), F32)
    for k in range(nbd):
        prod = total(slot[k * bsz : (k + 1) * bsz, :] * wt[:, k : k + 1])
        out += jnp.where(cio == codes[q, nbd + k, pl.ds(me_c, 1), :], prod, 0.0)
    return out


def col_peaks(nbd, cb, q, slot, codes):
    me_c = lax.axis_index("col")
    bsz = slot.shape[1]
    cio = iota((cb, bsz), 0).astype(F32)
    out = jnp.zeros((cb, bsz), F32)
    for k in range(nbd):
        peak = jnp.max(jnp.abs(slot[k * bsz : (k + 1) * bsz, :]), axis=0, keepdims=True)
        live = codes[q, k, pl.ds(me_c, 1), :] >= 0.0
        hit = (cio == codes[q, nbd + k, pl.ds(me_c, 1), :]) & live
        out = jnp.maximum(out, jnp.where(hit, peak, 0.0))
    return out


def scales_kernel(nbd, R, C, rb, cb, origins, g1, *refs):
    half = R // 2 + 1 if R > 1 else 1
    slots = refs[:half]
    dr, codes, packed, part, colmax, w_ref, wr = refs[half:]
    me_r = lax.axis_index("row")
    bsz = dr.shape[1]
    base = nbd * bsz
    rio = iota((rb, bsz), 0).astype(F32)
    wr[...] = jnp.zeros_like(wr)
    for q in range(R):
        meta = g1[q * C : (q + 1) * C, 0, base:]
        for k in range(2 * nbd):
            codes[q, k] = jnp.broadcast_to(meta[:, k : k + 1], (C, bsz))

        def body(c, acc):
            for k in range(nbd):
                hit = rio == codes[q, k, pl.ds(c, 1), :]
                acc = jnp.maximum(acc, jnp.where(hit, g1[q * C + c, :, k * bsz : (k + 1) * bsz], 0.0))
            return acc

        peak = lax.fori_loop(0, C, body, jnp.zeros((rb, bsz), F32), unroll=min(C, 8))
        dr[q * rb : (q + 1) * rb, :] = 1.0 / jnp.sqrt(jnp.maximum(peak, 0.5))
    share = iota((C, bsz), 1) // (bsz // C)
    mine = jnp.full((C, bsz), -1.0, F32)
    for k in range(nbd):
        mine = jnp.where(share == k, codes[me_r, k], mine)
    packed[...] = mine
    top = jnp.zeros((cb, bsz), F32)
    groups = [origins(me_r, s) for s in range(half)]
    for q, slot in zip(groups, slots):
        at = pl.ds(pl.multiple_of(q * rb, rb), rb)
        w_ref[at, :] = dr[at, :] * slot[base : base + rb, :]
        top = jnp.maximum(top, col_peaks(nbd, cb, q, slot, codes))
    colmax[...] = top
    wt = weights(nbd, rb, groups, codes, w_ref, wr)
    for s, (q, slot) in enumerate(zip(groups, slots)):
        part[q] = backward(nbd, cb, q, slot, codes, wt[:, s * nbd : (s + 1) * nbd])


def primal_kernel(nbd, R, C, rb, cb, origins, *refs):
    half = R // 2 + 1 if R > 1 else 1
    slots, own = refs[: R - half], refs[R - half]
    aux, dr, codes, done, colmax, x_new, dc, p3, w_ref, wr, part = refs[R - half + 1 :]
    me_r = lax.axis_index("row")
    me_c = lax.axis_index("col")
    bsz = x_new.shape[1]
    base = nbd * bsz
    x_prev, cost, upper = (aux[i * cb : (i + 1) * cb, :] for i in range(3))
    eta, omega = (aux[3 * cb + i : 3 * cb + i + 1, :] for i in range(2))
    cio = iota((cb, bsz), 0).astype(F32)
    wr[...] = jnp.zeros_like(wr)
    top = colmax[...]
    for s in range(half):
        q = origins(me_r, s)
        part[q] = done[q]
    groups = [origins(me_r, s) for s in range(half, R)]
    for q, slot in zip(groups, slots):
        at = pl.ds(pl.multiple_of(q * rb, rb), rb)
        w_ref[at, :] = dr[at, :] * slot[base : base + rb, :]
        top = jnp.maximum(top, col_peaks(nbd, cb, q, slot, codes))
    wt = weights(nbd, rb, groups, codes, w_ref, wr)
    for s, (q, slot) in enumerate(zip(groups, slots)):
        part[q] = backward(nbd, cb, q, slot, codes, wt[:, s * nbd : (s + 1) * nbd])
    got = part[0]
    for q in range(1, R):
        got += part[q]
    scale = 1.0 / jnp.sqrt(jnp.maximum(top, 0.5))
    dc[...] = scale
    grad = scale * cost - got * scale
    xn = jnp.clip(x_prev - eta / omega * grad, 0.0, upper / scale)
    x_new[...] = xn
    v2 = scale * (xn - x_prev)
    v1 = scale * xn + v2
    both, step = [], []
    for k in range(nbd):
        a = own[k * bsz : (k + 1) * bsz, :]
        hit = cio == codes[me_r, nbd + k, pl.ds(me_c, 1), :]
        for v, out in ((v1, both), (v2, step)):
            out.append(jnp.sum(a * total(jnp.where(hit, v, 0.0)), axis=1, keepdims=True))
    rows = rows_of(both + step, bsz)
    lanes = bsz // C
    share = iota((C, bsz), 1) // lanes
    row = jnp.zeros((C, bsz), F32)
    for k in range(nbd):
        part_k = pltpu.roll(rows[nbd + k : nbd + k + 1, :], (k + 1) * lanes % bsz, 1)
        part_k = jnp.broadcast_to(part_k, (C, bsz))
        part_k = pltpu.roll(part_k, 0, 1, stride=lanes, stride_axis=0)
        row = jnp.where(share == k, part_k, row)
        p3[:, :, k * bsz : (k + 1) * bsz] = jnp.broadcast_to(
            rows[k : k + 1, :][None], (p3.shape[0], 1, bsz)
        )
    for q in range(R):
        p3[q * C : (q + 1) * C, 0, base:] = row


def dual_kernel(nbd, R, C, rb, cb, origins, g3, *refs):
    slots = refs[:R]
    aux, dr, codes, packed, x_new, dc, y_new, p4, dual, w_ref, wr, part = refs[R:]
    me_r = lax.axis_index("row")
    me_c = lax.axis_index("col")
    bsz = x_new.shape[1]
    base = nbd * bsz
    x_prev, cost, upper = (aux[i * cb : (i + 1) * cb, :] for i in range(3))
    eta, omega = (aux[3 * cb + i : 3 * cb + i + 1, :] for i in range(2))
    rio = iota((rb, bsz), 0).astype(F32)
    wr[...] = jnp.zeros_like(wr)
    sigma = eta * omega
    for s, slot in enumerate(slots):
        q = origins(me_r, s)
        at = pl.ds(pl.multiple_of(q * rb, rb), rb)

        def body(c, acc):
            for k in range(nbd):
                hit = rio == codes[q, k, pl.ds(c, 1), :]
                acc = acc + jnp.where(hit, g3[q * C + c, :, k * bsz : (k + 1) * bsz], 0.0)
            return acc

        both = lax.fori_loop(0, C, body, jnp.zeros((rb, bsz), F32), unroll=min(C, 8))
        scale = dr[at, :]
        both = both * scale
        bs = scale * slot[base + rb : base + 2 * rb, :]
        yp = slot[base : base + rb, :]
        yn = yp + sigma * (bs - both)
        w_ref[at, :] = scale * yn
        dy = yn - yp
        part[q, 0:1, :] = total(dy * dy)
        part[q, 1:2, :] = total(bs * yn)
        if s == 0:
            y_new[...] = yn

            def mine(c, acc):
                hit = rio == packed[pl.ds(c, 1), :]
                return acc + jnp.where(hit, g3[q * C + c, :, base:], 0.0)

            shares = lax.fori_loop(0, C, mine, jnp.zeros((rb, bsz), F32), unroll=min(C, 8))
            lanes = bsz // C
            adx = shares
            for k in range(1, nbd):
                adx = adx + pltpu.roll(shares, bsz - k * lanes, 1)
            adx = pltpu.roll(adx, (C - 1 - me_c) * lanes, 1) * scale
            inside = iota((rb, bsz), 1) // lanes == C - 1 - me_c
            adx = jnp.where(inside, adx, 0.0)
            resid = jnp.where(inside, bs - (both - adx), 0.0)
            adx2 = total(adx * adx)
            res2 = total(resid * resid)
    sums = part[0, :2, :]
    for q in range(1, R):
        sums += part[q, :2, :]
    dual[:2, :] = jnp.broadcast_to(jnp.sum(sums, axis=1, keepdims=True), (2, bsz))
    dual[2:, :] = jnp.broadcast_to(omega, (6, bsz))
    groups = [origins(me_r, s) for s in range(R)]
    wt = weights(nbd, rb, groups, codes, w_ref, wr)
    for s, (q, slot) in enumerate(zip(groups, slots)):
        part[q] = backward(nbd, cb, q, slot, codes, wt[:, s * nbd : (s + 1) * nbd])
    got = part[0]
    for q in range(1, R):
        got += part[q]
    scale = dc[...]
    cs = scale * cost
    reduced = cs - got * scale
    us = upper / scale
    xn = x_new[...]
    dx = xn - x_prev
    terms = [total(dx * dx), total(cs * xn), total(us * jnp.maximum(-reduced, 0.0)), adx2, res2]
    sub, lane = iota((8, bsz), 0), iota((8, bsz), 1)
    stack = jnp.zeros((8, bsz), F32)
    for i, term in enumerate(terms):
        stack = jnp.where(sub == i, term, stack)
    sums = jnp.sum(stack, axis=1, keepdims=True)
    out = total(jnp.where(sub == lane, sums, 0.0))
    p4[...] = jnp.broadcast_to(out[None], p4.shape)


def stats_kernel(C, total_rows, total_cols, g4, dual, x_new, y_new, stats, x_out, y_out, last, sems):
    outs = [
        pltpu.make_async_copy(a, b, sems.at[i])
        for i, (a, b) in enumerate(((x_new, x_out), (y_new, y_out), (last, stats)))
    ]
    outs[0].start()
    outs[1].start()
    bsz = g4.shape[2]
    sums = g4[0]
    for c in range(1, C):
        sums += g4[c]
    every = sums
    for d in range(C, g4.shape[0]):
        every += g4[d]
    sub, lane = iota((8, bsz), 0), iota((8, bsz), 1)
    stack = jnp.where(lane < 3, sums, every)
    stack = jnp.broadcast_to(
        jnp.sum(jnp.where(sub == lane, stack, 0.0), axis=1, keepdims=True), (8, bsz)
    )
    dx2, cx, uneg, adx2, res2 = (stack[i : i + 1, :] for i in range(5))
    dy2, by = (dual[i : i + 1, :] for i in range(2))
    lane = lane[:1]
    omega = dual[2:3, :]
    movement = 0.5 * omega * dx2 + 0.5 / omega * dy2
    first = jnp.sqrt(res2 / total_rows)
    second = (cx - by + uneg) / total_cols
    third = movement / jnp.sqrt(adx2 * dy2 + 1e-06)
    out = jnp.where(lane == 0, first, jnp.where(lane == 1, second, third))
    last[...] = out[:, : last.shape[1]]
    outs[2].start()
    for copy in outs:
        copy.wait()


def shards(blocks, block_rows, block_cols, counts, x_prev, y_prev, cost, rhs, upper, steps):
    R = lax.axis_size("row")
    C = lax.axis_size("col")
    ndev = R * C
    nbd, bsz = blocks.shape[2], blocks.shape[3]
    rb = y_prev.shape[0] // bsz
    cb = x_prev.shape[0] // bsz
    half = R // 2 + 1 if R > 1 else 1
    in_hbm = functools.partial(pltpu.with_memory_space_constraint, memory_space=pltpu.HBM)
    shape = lambda *dims: jax.ShapeDtypeStruct(dims, F32)
    params = pltpu.CompilerParams(vmem_limit_bytes=LIMIT)
    raw = (
        blocks[0, 0],
        y_prev.reshape(rb, bsz),
        rhs.reshape(rb, bsz),
        x_prev.reshape(cb, bsz),
        cost.reshape(cb, bsz),
        upper.reshape(cb, bsz),
        block_rows,
        block_cols,
        steps,
    )
    p1, bulk, aux = pl.pallas_call(
        functools.partial(peaks_kernel, nbd),
        out_shape=(
            shape(ndev, 1, (nbd + 1) * bsz),
            shape(nbd * bsz + 2 * rb, bsz),
            shape(3 * cb + 8, bsz),
        ),
        in_specs=[HBM] * len(raw) + [SMEM],
        out_specs=(VMEM,) * 3,
        scratch_shapes=[
            pltpu.SMEM((1, 1, nbd), jnp.int32),
            pltpu.SMEM((1, 1, nbd), jnp.int32),
            pltpu.SMEM(steps.shape, F32),
            pltpu.SemaphoreType.DMA((nbd + 8,)),
        ],
        compiler_params=params,
        name="peaks",
    )(*map(in_hbm, raw), counts)

    def spread(v):
        return lax.all_to_all(v, ("row", "col"), 0, 0, tiled=True)

    def swap(v, step):
        return lax.ppermute(v, "row", [(i, i ^ step) for i in range(R)])

    far, far_ids, step = [bulk], [0], R // 2
    while step > 1:
        far += [swap(v, step) for v in far]
        far_ids += [i ^ step for i in far_ids]
        step //= 2
    slots, ids = far[:1], [0]
    if R > 1:
        slots.append(swap(bulk, 1))
        ids.append(1)
    g1 = spread(p1)
    g1, slots[-1], *far = lax.optimization_barrier((g1, slots[-1], *far[1:]))
    slots += far + [swap(v, 1) for v in far]
    ids += far_ids[1:] + [i ^ 1 for i in far_ids[1:]]

    def origins(me, s):
        return me ^ ids[s] if ids[s] else me

    scratch = [
        pltpu.VMEM((R * rb, bsz), F32),
        pltpu.VMEM((up(R * nbd, bsz), bsz), F32),
    ]
    part = pltpu.VMEM((R, up(cb, 8), bsz), F32)
    sizes = (nbd, R, C, rb, cb, origins)
    dr, codes, packed, done, colmax = pl.pallas_call(
        functools.partial(scales_kernel, *sizes),
        out_shape=(
            shape(R * rb, bsz),
            shape(R, 2 * nbd, C, bsz),
            shape(C, bsz),
            shape(R, cb, bsz),
            shape(cb, bsz),
        ),
        in_specs=[VMEM] * (1 + half),
        out_specs=(VMEM,) * 5,
        scratch_shapes=scratch,
        compiler_params=params,
        name="scales",
    )(g1, *slots[:half])
    x_new, dc, p3 = pl.pallas_call(
        functools.partial(primal_kernel, *sizes),
        out_shape=(shape(cb, bsz), shape(cb, bsz), shape(ndev, 1, (nbd + 1) * bsz)),
        in_specs=[VMEM] * (R - half + 6),
        out_specs=(VMEM,) * 3,
        scratch_shapes=scratch + [part],
        compiler_params=params,
        name="primal",
    )(*slots[half:], bulk, aux, dr, codes, done, colmax)
    g3 = spread(p3)
    y_new, p4, dual = pl.pallas_call(
        functools.partial(dual_kernel, *sizes),
        out_shape=(shape(rb, bsz), shape(ndev, 1, bsz), shape(8, bsz)),
        in_specs=[VMEM] * (R + 7),
        out_specs=(VMEM,) * 3,
        scratch_shapes=scratch + [part],
        compiler_params=params,
        name="dual",
    )(g3, *slots, aux, dr, codes, packed, x_new, dc)
    g4 = spread(p4)
    stats, x_new, y_new = pl.pallas_call(
        functools.partial(
            stats_kernel, C, float(y_prev.shape[0] * R), float(x_prev.shape[0] * C)
        ),
        out_shape=(shape(1, 3), shape(cb, bsz), shape(rb, bsz)),
        in_specs=[VMEM] * 4,
        out_specs=(HBM,) * 3,
        scratch_shapes=[pltpu.VMEM((1, 3), F32), pltpu.SemaphoreType.DMA((3,))],
        compiler_params=params,
        name="stats",
    )(g4, dual, x_new, y_new)
    return (x_new.reshape(-1), y_new.reshape(-1), stats.reshape(-1))


def solution(mesh):
    placed = (
        P("row", "col", None, None, None),
        P("row", "col", None),
        P("row", "col", None),
        P("row", "col"),
        P("col"),
        P("row"),
        P("col"),
        P("row"),
        P("col"),
        P(),
    )
    return jax.shard_map(
        shards, mesh=mesh, in_specs=placed, out_specs=(P("col"), P("row"), P()), check_vma=False
    )
```

```python
import functools

import jax
import jax.numpy as jnp
from jax import lax
from jax.experimental import pallas as pl
from jax.experimental.pallas import tpu as pltpu
from jax.sharding import PartitionSpec as P

F32 = jnp.float32
VMEM = pl.BlockSpec(memory_space=pltpu.VMEM)
SMEM = pl.BlockSpec(memory_space=pltpu.SMEM)
HBM = pl.BlockSpec(memory_space=pltpu.HBM)
LIMIT = 40 * 1024 * 1024
SPLITS = 3


def up(n, m):
    return -(-n // m) * m


def iota(shape, dim):
    return lax.broadcasted_iota(jnp.int32, shape, dim)


def total(rows):
    return jnp.sum(rows, axis=0, keepdims=True)


def peaks_kernel(nbd, blocks, y, rhs, x, cost, upper, brow, bcol, steps, count, p1, bulk, aux, turned, *scratch):
    s_row, s_col, s_steps, sems = scratch
    bsz = bulk.shape[1]
    rb = y.shape[0]
    cb = x.shape[0]
    base = nbd * bsz
    pairs = [
        (blocks, bulk.at[:base]),
        (brow, s_row),
        (bcol, s_col),
        (steps, s_steps),
        (y, bulk.at[base : base + rb]),
        (rhs, bulk.at[base + rb : base + 2 * rb]),
        (x, aux.at[:cb]),
        (cost, aux.at[cb : 2 * cb]),
        (upper, aux.at[2 * cb : 3 * cb]),
    ]
    loads = [pltpu.make_async_copy(a, b, sems.at[i]) for i, (a, b) in enumerate(pairs)]
    for copy in loads:
        copy.start()
    loads[0].wait()
    peaks = []
    for k in range(nbd):
        a = bulk[k * bsz : (k + 1) * bsz, :]
        a = a.T
        turned[k * bsz : (k + 1) * bsz, :] = a
        peaks.append(jnp.max(jnp.abs(a), axis=0, keepdims=True))
    for copy in loads[1:]:
        copy.wait()
    lane = iota((1, bsz), 1)
    meta = jnp.full((1, bsz), -1.0, F32)
    for k in range(nbd):
        code = jnp.where(k < count[0, 0], s_row[0, 0, k], -1).astype(F32)
        meta = jnp.where(lane == k, code, meta)
        meta = jnp.where(lane == nbd + k, s_col[0, 0, k].astype(F32), meta)
    for k, piece in enumerate(peaks + [meta]):
        p1[:, :, k * bsz : (k + 1) * bsz] = jnp.broadcast_to(piece[None], (p1.shape[0], 1, bsz))
    asub = iota((8, bsz), 0)
    aux[3 * cb :, :] = jnp.where(asub == 0, s_steps[0], s_steps[1])


def split(v):
    parts = []
    for _ in range(SPLITS):
        top = v.astype(jnp.bfloat16).astype(F32)
        parts.append(top)
        v = v - top
    return parts


def split_blocks(nbd, slot, out):
    bsz = slot.shape[1]
    for k in range(nbd):
        at = slice(k * bsz, (k + 1) * bsz)
        for i, v in enumerate(split(slot[at, :])):
            out[i, at, :] = v.astype(jnp.bfloat16)


def product(left, right, dims):
    n = left.shape[0]
    left = jnp.concatenate(split(left), axis=0).astype(jnp.bfloat16)
    out = 0.0
    for j in range(SPLITS):
        got = lax.dot_general(left, right(j), (dims, ((), ())), preferred_element_type=F32)
        for i in range(SPLITS - j):
            out = out + got[i * n : (i + 1) * n]
    return out


def backward(nbd, rb, cb, q, parts, codes, w_ref):
    me_c = lax.axis_index("col")
    bsz = w_ref.shape[1]
    rio = iota((rb, bsz), 0).astype(F32)
    cio = iota((cb, bsz), 0).astype(F32)
    w = w_ref[pl.ds(pl.multiple_of(q * rb, rb), rb), :]
    picks = []
    for k in range(nbd):
        row = total(jnp.where(rio == codes[q, k, pl.ds(me_c, 1), :], w, 0.0))
        picks.append(jnp.where(cio == codes[q, nbd + k, pl.ds(me_c, 1), :], row, 0.0))
    return product(jnp.concatenate(picks, axis=1), lambda i: parts[i], ((1,), (0,)))


def col_peaks(nbd, cb, q, slot, codes):
    me_c = lax.axis_index("col")
    bsz = slot.shape[1]
    cio = iota((cb, bsz), 0).astype(F32)
    out = jnp.zeros((cb, bsz), F32)
    for k in range(nbd):
        peak = jnp.max(jnp.abs(slot[k * bsz : (k + 1) * bsz, :]), axis=0, keepdims=True)
        live = codes[q, k, pl.ds(me_c, 1), :] >= 0.0
        hit = (cio == codes[q, nbd + k, pl.ds(me_c, 1), :]) & live
        out = jnp.maximum(out, jnp.where(hit, peak, 0.0))
    return out


def scales_kernel(nbd, R, C, rb, cb, origins, g1, turned, *refs):
    half = R // 2 + 1 if R > 1 else 1
    slots = refs[:half]
    dr, codes, packed, part, colmax, parts, own, w_ref = refs[half:]
    me_r = lax.axis_index("row")
    bsz = dr.shape[1]
    base = nbd * bsz
    rio = iota((rb, bsz), 0).astype(F32)
    for q in range(R):
        meta = g1[q * C : (q + 1) * C, 0, base:]
        for k in range(2 * nbd):
            codes[q, k] = jnp.broadcast_to(meta[:, k : k + 1], (C, bsz))

        def body(c, acc):
            for k in range(nbd):
                hit = rio == codes[q, k, pl.ds(c, 1), :]
                acc = jnp.maximum(acc, jnp.where(hit, g1[q * C + c, :, k * bsz : (k + 1) * bsz], 0.0))
            return acc

        peak = lax.fori_loop(0, C, body, jnp.zeros((rb, bsz), F32), unroll=min(C, 8))
        dr[q * rb : (q + 1) * rb, :] = 1.0 / jnp.sqrt(jnp.maximum(peak, 0.5))
    share = iota((C, bsz), 1) // (bsz // C)
    mine = jnp.full((C, bsz), -1.0, F32)
    for k in range(nbd):
        mine = jnp.where(share == k, codes[me_r, k], mine)
    packed[...] = mine
    top = jnp.zeros((cb, bsz), F32)
    groups = [origins(me_r, s) for s in range(half)]
    for q, slot in zip(groups, slots):
        at = pl.ds(pl.multiple_of(q * rb, rb), rb)
        w_ref[at, :] = dr[at, :] * slot[base : base + rb, :]
        top = jnp.maximum(top, col_peaks(nbd, cb, q, slot, codes))
    colmax[...] = top
    for s, (q, slot) in enumerate(zip(groups, slots)):
        split_blocks(nbd, slot, parts.at[s])
        part[q] = backward(nbd, rb, cb, q, parts.at[s], codes, w_ref)
    split_blocks(nbd, turned, own)


def primal_kernel(nbd, R, C, rb, cb, origins, *refs):
    half = R // 2 + 1 if R > 1 else 1
    slots, own = refs[: R - half], refs[R - half]
    aux, dr, codes, done, colmax, x_new, dc, p3, parts, w_ref, part = refs[R - half + 1 :]
    me_r = lax.axis_index("row")
    me_c = lax.axis_index("col")
    bsz = x_new.shape[1]
    base = nbd * bsz
    x_prev, cost, upper = (aux[i * cb : (i + 1) * cb, :] for i in range(3))
    eta, omega = (aux[3 * cb + i : 3 * cb + i + 1, :] for i in range(2))
    cio = iota((cb, bsz), 0).astype(F32)
    top = colmax[...]
    for s in range(half):
        q = origins(me_r, s)
        part[q] = done[q]
    groups = [origins(me_r, s) for s in range(half, R)]
    for q, slot in zip(groups, slots):
        at = pl.ds(pl.multiple_of(q * rb, rb), rb)
        w_ref[at, :] = dr[at, :] * slot[base : base + rb, :]
        top = jnp.maximum(top, col_peaks(nbd, cb, q, slot, codes))
    for s, (q, slot) in enumerate(zip(groups, slots)):
        split_blocks(nbd, slot, parts.at[s])
        part[q] = backward(nbd, rb, cb, q, parts.at[s], codes, w_ref)
    got = part[0]
    for q in range(1, R):
        got += part[q]
    scale = 1.0 / jnp.sqrt(jnp.maximum(top, 0.5))
    dc[...] = scale
    grad = scale * cost - got * scale
    xn = jnp.clip(x_prev - eta / omega * grad, 0.0, upper / scale)
    x_new[...] = xn
    v2 = scale * (xn - x_prev)
    v1 = scale * xn + v2
    sub = iota((up(2 * nbd, 8), bsz), 0)
    picks = []
    for k in range(nbd):
        hit = cio == codes[me_r, nbd + k, pl.ds(me_c, 1), :]
        one, two = (total(jnp.where(hit, v, 0.0)) for v in (v1, v2))
        picks.append(jnp.where(sub == k, one, jnp.where(sub == nbd + k, two, 0.0)))
    rows = product(jnp.concatenate(picks, axis=1), lambda i: own[i], ((1,), (0,)))
    lanes = bsz // C
    turn = (iota((C, bsz), 1) // lanes + iota((C, bsz), 0)) % C
    row = jnp.zeros((C, bsz), F32)
    for k in range(nbd):
        part_k = pltpu.roll(rows[nbd + k : nbd + k + 1, :], (k + 1) * lanes % bsz, 1)
        row = jnp.where(turn == k, part_k, row)
        p3[:, :, k * bsz : (k + 1) * bsz] = jnp.broadcast_to(
            rows[k : k + 1, :][None], (p3.shape[0], 1, bsz)
        )
    row = pltpu.roll(row, 0, 1, stride=lanes, stride_axis=0)
    for q in range(R):
        p3[q * C : (q + 1) * C, 0, base:] = row


def dual_kernel(nbd, R, C, rb, cb, origins, g3, *refs):
    slots = refs[:R]
    early, late, aux, dr, codes, packed, x_new, dc, y_new, p4, dual, w_ref, part = refs[R:]
    me_r = lax.axis_index("row")
    me_c = lax.axis_index("col")
    bsz = x_new.shape[1]
    base = nbd * bsz
    x_prev, cost, upper = (aux[i * cb : (i + 1) * cb, :] for i in range(3))
    eta, omega = (aux[3 * cb + i : 3 * cb + i + 1, :] for i in range(2))
    rio = iota((rb, bsz), 0).astype(F32)
    sigma = eta * omega
    for s, slot in enumerate(slots):
        q = origins(me_r, s)
        at = pl.ds(pl.multiple_of(q * rb, rb), rb)

        def body(c, acc):
            for k in range(nbd):
                hit = rio == codes[q, k, pl.ds(c, 1), :]
                acc = acc + jnp.where(hit, g3[q * C + c, :, k * bsz : (k + 1) * bsz], 0.0)
            return acc

        both = lax.fori_loop(0, C, body, jnp.zeros((rb, bsz), F32), unroll=min(C, 8))
        scale = dr[at, :]
        both = both * scale
        bs = scale * slot[base + rb : base + 2 * rb, :]
        yp = slot[base : base + rb, :]
        yn = yp + sigma * (bs - both)
        w_ref[at, :] = scale * yn
        dy = yn - yp
        part[q, 0:1, :] = total(dy * dy)
        part[q, 1:2, :] = total(bs * yn)
        if s == 0:
            y_new[...] = yn

            def mine(c, acc):
                hit = rio == packed[pl.ds(c, 1), :]
                return acc + jnp.where(hit, g3[q * C + c, :, base:], 0.0)

            shares = lax.fori_loop(0, C, mine, jnp.zeros((rb, bsz), F32), unroll=min(C, 8))
            lanes = bsz // C
            adx = shares
            for k in range(1, nbd):
                adx = adx + pltpu.roll(shares, bsz - k * lanes, 1)
            adx = pltpu.roll(adx, (C - 1 - me_c) * lanes, 1) * scale
            inside = iota((rb, bsz), 1) // lanes == C - 1 - me_c
            adx = jnp.where(inside, adx, 0.0)
            resid = jnp.where(inside, bs - (both - adx), 0.0)
            adx2 = total(adx * adx)
            res2 = total(resid * resid)
    sums = part[0, :2, :]
    for q in range(1, R):
        sums += part[q, :2, :]
    dual[:2, :] = jnp.broadcast_to(jnp.sum(sums, axis=1, keepdims=True), (2, bsz))
    dual[2:, :] = jnp.broadcast_to(omega, (6, bsz))
    groups = [origins(me_r, s) for s in range(R)]
    half = early.shape[0]
    for s, q in enumerate(groups):
        parts = early.at[s] if s < half else late.at[s - half]
        part[q] = backward(nbd, rb, cb, q, parts, codes, w_ref)
    got = part[0]
    for q in range(1, R):
        got += part[q]
    scale = dc[...]
    cs = scale * cost
    reduced = cs - got * scale
    us = upper / scale
    xn = x_new[...]
    dx = xn - x_prev
    terms = [total(dx * dx), total(cs * xn), total(us * jnp.maximum(-reduced, 0.0)), adx2, res2]
    sub, lane = iota((8, bsz), 0), iota((8, bsz), 1)
    stack = jnp.zeros((8, bsz), F32)
    for i, term in enumerate(terms):
        stack = jnp.where(sub == i, term, stack)
    sums = jnp.sum(stack, axis=1, keepdims=True)
    out = total(jnp.where(sub == lane, sums, 0.0))
    p4[...] = jnp.broadcast_to(out[None], p4.shape)


def stats_kernel(C, total_rows, total_cols, g4, dual, x_new, y_new, stats, x_out, y_out, last, sems):
    outs = [
        pltpu.make_async_copy(a, b, sems.at[i])
        for i, (a, b) in enumerate(((x_new, x_out), (y_new, y_out), (last, stats)))
    ]
    outs[0].start()
    outs[1].start()
    bsz = g4.shape[2]
    sums = g4[0]
    for c in range(1, C):
        sums += g4[c]
    every = sums
    for d in range(C, g4.shape[0]):
        every += g4[d]
    sub, lane = iota((8, bsz), 0), iota((8, bsz), 1)
    stack = jnp.where(lane < 3, sums, every)
    stack = jnp.broadcast_to(
        jnp.sum(jnp.where(sub == lane, stack, 0.0), axis=1, keepdims=True), (8, bsz)
    )
    dx2, cx, uneg, adx2, res2 = (stack[i : i + 1, :] for i in range(5))
    dy2, by = (dual[i : i + 1, :] for i in range(2))
    lane = lane[:1]
    omega = dual[2:3, :]
    movement = 0.5 * omega * dx2 + 0.5 / omega * dy2
    first = jnp.sqrt(res2 / total_rows)
    second = (cx - by + uneg) / total_cols
    third = movement / jnp.sqrt(adx2 * dy2 + 1e-06)
    out = jnp.where(lane == 0, first, jnp.where(lane == 1, second, third))
    last[...] = out[:, : last.shape[1]]
    outs[2].start()
    for copy in outs:
        copy.wait()


def shards(blocks, block_rows, block_cols, counts, x_prev, y_prev, cost, rhs, upper, steps):
    R = lax.axis_size("row")
    C = lax.axis_size("col")
    ndev = R * C
    nbd, bsz = blocks.shape[2], blocks.shape[3]
    rb = y_prev.shape[0] // bsz
    cb = x_prev.shape[0] // bsz
    half = R // 2 + 1 if R > 1 else 1
    in_hbm = functools.partial(pltpu.with_memory_space_constraint, memory_space=pltpu.HBM)
    shape = lambda *dims: jax.ShapeDtypeStruct(dims, F32)
    params = pltpu.CompilerParams(vmem_limit_bytes=LIMIT)
    raw = (
        blocks.reshape(nbd * bsz, bsz),
        y_prev.reshape(rb, bsz),
        rhs.reshape(rb, bsz),
        x_prev.reshape(cb, bsz),
        cost.reshape(cb, bsz),
        upper.reshape(cb, bsz),
        block_rows,
        block_cols,
        steps,
    )
    p1, bulk, aux, turned = pl.pallas_call(
        functools.partial(peaks_kernel, nbd),
        out_shape=(
            shape(ndev, 1, (nbd + 1) * bsz),
            shape(nbd * bsz + 2 * rb, bsz),
            shape(3 * cb + 8, bsz),
            shape(nbd * bsz, bsz),
        ),
        in_specs=[HBM] * len(raw) + [SMEM],
        out_specs=(VMEM,) * 4,
        scratch_shapes=[
            pltpu.SMEM((1, 1, nbd), jnp.int32),
            pltpu.SMEM((1, 1, nbd), jnp.int32),
            pltpu.SMEM(steps.shape, F32),
            pltpu.SemaphoreType.DMA((9,)),
        ],
        compiler_params=params,
        name="peaks",
    )(*map(in_hbm, raw), counts)

    def spread(v):
        return lax.all_to_all(v, ("row", "col"), 0, 0, tiled=True)

    def swap(v, step):
        return lax.ppermute(v, "row", [(i, i ^ step) for i in range(R)])

    far, far_ids, step = [bulk], [0], R // 2
    while step > 1:
        far += [swap(v, step) for v in far]
        far_ids += [i ^ step for i in far_ids]
        step //= 2
    slots, ids = far[:1], [0]
    if R > 1:
        slots.append(swap(bulk, 1))
        ids.append(1)
    g1 = spread(p1)
    g1, slots[-1], *far = lax.optimization_barrier((g1, slots[-1], *far[1:]))
    slots += far + [swap(v, 1) for v in far]
    ids += far_ids[1:] + [i ^ 1 for i in far_ids[1:]]

    def origins(me, s):
        return me ^ ids[s] if ids[s] else me

    scratch = [pltpu.VMEM((R * rb, bsz), F32)]

    def parts_of(n):
        return jax.ShapeDtypeStruct((n, SPLITS, nbd * bsz, bsz), jnp.bfloat16)

    part = pltpu.VMEM((R, up(cb, 8), bsz), F32)
    sizes = (nbd, R, C, rb, cb, origins)
    dr, codes, packed, done, colmax, early, own = pl.pallas_call(
        functools.partial(scales_kernel, *sizes),
        out_shape=(
            shape(R * rb, bsz),
            shape(R, 2 * nbd, C, bsz),
            shape(C, bsz),
            shape(R, cb, bsz),
            shape(cb, bsz),
            parts_of(half),
            jax.ShapeDtypeStruct((SPLITS, nbd * bsz, bsz), jnp.bfloat16),
        ),
        in_specs=[VMEM] * (2 + half),
        out_specs=(VMEM,) * 7,
        scratch_shapes=scratch,
        compiler_params=params,
        name="scales",
    )(g1, turned, *slots[:half])
    x_new, dc, p3, late = pl.pallas_call(
        functools.partial(primal_kernel, *sizes),
        out_shape=(
            shape(cb, bsz),
            shape(cb, bsz),
            shape(ndev, 1, (nbd + 1) * bsz),
            parts_of(max(R - half, 1)),
        ),
        in_specs=[VMEM] * (R - half + 6),
        out_specs=(VMEM,) * 4,
        scratch_shapes=scratch + [part],
        compiler_params=params,
        name="primal",
    )(*slots[half:], own, aux, dr, codes, done, colmax)
    g3 = spread(p3)
    y_new, p4, dual = pl.pallas_call(
        functools.partial(dual_kernel, *sizes),
        out_shape=(shape(rb, bsz), shape(ndev, 1, bsz), shape(8, bsz)),
        in_specs=[VMEM] * (R + 9),
        out_specs=(VMEM,) * 3,
        scratch_shapes=scratch + [part],
        compiler_params=params,
        name="dual",
    )(g3, *slots, early, late, aux, dr, codes, packed, x_new, dc)
    g4 = spread(p4)
    stats, x_new, y_new = pl.pallas_call(
        functools.partial(
            stats_kernel, C, float(y_prev.shape[0] * R), float(x_prev.shape[0] * C)
        ),
        out_shape=(shape(1, 3), shape(cb, bsz), shape(rb, bsz)),
        in_specs=[VMEM] * 4,
        out_specs=(HBM,) * 3,
        scratch_shapes=[pltpu.VMEM((1, 3), F32), pltpu.SemaphoreType.DMA((3,))],
        compiler_params=params,
        name="stats",
    )(g4, dual, x_new, y_new)
    return (x_new.reshape(-1), y_new.reshape(-1), stats.reshape(-1))


def solution(mesh):
    placed = (
        P("row", "col", None, None, None),
        P("row", "col", None),
        P("row", "col", None),
        P("row", "col"),
        P("col"),
        P("row"),
        P("col"),
        P("row"),
        P("col"),
        P(),
    )
    return jax.shard_map(
        shards, mesh=mesh, in_specs=placed, out_specs=(P("col"), P("row"), P()), check_vma=False
    )
```

```python
import functools

import jax
import jax.numpy as jnp
from jax import lax
from jax.experimental import pallas as pl
from jax.experimental.pallas import tpu as pltpu
from jax.sharding import PartitionSpec as P

F32 = jnp.float32
VMEM = pl.BlockSpec(memory_space=pltpu.VMEM)
SMEM = pl.BlockSpec(memory_space=pltpu.SMEM)
HBM = pl.BlockSpec(memory_space=pltpu.HBM)
LIMIT = 40 * 1024 * 1024
SPLITS = 3


def up(n, m):
    return -(-n // m) * m


def iota(shape, dim):
    return lax.broadcasted_iota(jnp.int32, shape, dim)


def total(rows):
    return jnp.sum(rows, axis=0, keepdims=True)


def peaks_kernel(nbd, blocks, y, rhs, x, cost, upper, brow, bcol, steps, count, p1, bulk, aux, turned, *scratch):
    s_row, s_col, s_steps, sems = scratch
    bsz = bulk.shape[1]
    rb = y.shape[0]
    cb = x.shape[0]
    base = nbd * bsz
    pairs = [
        (blocks, bulk.at[:base]),
        (brow, s_row),
        (bcol, s_col),
        (steps, s_steps),
        (y, bulk.at[base : base + rb]),
        (rhs, bulk.at[base + rb : base + 2 * rb]),
        (x, aux.at[:cb]),
        (cost, aux.at[cb : 2 * cb]),
        (upper, aux.at[2 * cb : 3 * cb]),
    ]
    loads = [pltpu.make_async_copy(a, b, sems.at[i]) for i, (a, b) in enumerate(pairs)]
    for copy in loads:
        copy.start()
    loads[0].wait()
    peaks = []
    for k in range(nbd):
        a = bulk[k * bsz : (k + 1) * bsz, :]
        a = a.T
        turned[k * bsz : (k + 1) * bsz, :] = a
        peaks.append(jnp.max(jnp.abs(a), axis=0, keepdims=True))
    for copy in loads[1:]:
        copy.wait()
    lane = iota((1, bsz), 1)
    meta = jnp.full((1, bsz), -1.0, F32)
    for k in range(nbd):
        code = jnp.where(k < count[0, 0], s_row[0, 0, k], -1).astype(F32)
        meta = jnp.where(lane == k, code, meta)
        meta = jnp.where(lane == nbd + k, s_col[0, 0, k].astype(F32), meta)
    for k, piece in enumerate(peaks + [meta]):
        p1[:, :, k * bsz : (k + 1) * bsz] = jnp.broadcast_to(piece[None], (p1.shape[0], 1, bsz))
    asub = iota((8, bsz), 0)
    aux[3 * cb :, :] = jnp.where(asub == 0, s_steps[0], s_steps[1])


def split(v):
    parts = []
    most = float(jnp.finfo(jnp.bfloat16).max)
    for _ in range(SPLITS):
        top = v if parts else jnp.clip(v, -most, most)
        top = top.astype(jnp.bfloat16).astype(F32)
        parts.append(top)
        v = v - top
    return parts


def split_blocks(nbd, slot, out):
    bsz = slot.shape[1]
    for k in range(nbd):
        at = slice(k * bsz, (k + 1) * bsz)
        for i, v in enumerate(split(slot[at, :])):
            out[i, at, :] = v.astype(jnp.bfloat16)


def product(left, right, dims):
    n = left.shape[0]
    left = jnp.concatenate(split(left), axis=0).astype(jnp.bfloat16)
    out = 0.0
    for j in range(SPLITS):
        got = lax.dot_general(left, right(j), (dims, ((), ())), preferred_element_type=F32)
        for i in range(SPLITS - j):
            out = out + got[i * n : (i + 1) * n]
    return out


def backward(nbd, rb, cb, q, parts, codes, w_ref):
    me_c = lax.axis_index("col")
    bsz = w_ref.shape[1]
    rio = iota((rb, bsz), 0).astype(F32)
    cio = iota((cb, bsz), 0).astype(F32)
    w = w_ref[pl.ds(pl.multiple_of(q * rb, rb), rb), :]
    picks = []
    for k in range(nbd):
        row = total(jnp.where(rio == codes[q, k, pl.ds(me_c, 1), :], w, 0.0))
        picks.append(jnp.where(cio == codes[q, nbd + k, pl.ds(me_c, 1), :], row, 0.0))
    return product(jnp.concatenate(picks, axis=1), lambda i: parts[i], ((1,), (0,)))


def col_peaks(nbd, cb, q, slot, codes):
    me_c = lax.axis_index("col")
    bsz = slot.shape[1]
    cio = iota((cb, bsz), 0).astype(F32)
    out = jnp.zeros((cb, bsz), F32)
    for k in range(nbd):
        peak = jnp.max(jnp.abs(slot[k * bsz : (k + 1) * bsz, :]), axis=0, keepdims=True)
        live = codes[q, k, pl.ds(me_c, 1), :] >= 0.0
        hit = (cio == codes[q, nbd + k, pl.ds(me_c, 1), :]) & live
        out = jnp.maximum(out, jnp.where(hit, peak, 0.0))
    return out


def scales_kernel(nbd, R, C, rb, cb, origins, g1, turned, *refs):
    half = R // 2 + 1 if R > 1 else 1
    slots = refs[:half]
    dr, codes, packed, part, colmax, parts, own, w_ref = refs[half:]
    me_r = lax.axis_index("row")
    bsz = dr.shape[1]
    base = nbd * bsz
    rio = iota((rb, bsz), 0).astype(F32)
    for q in range(R):
        meta = g1[q * C : (q + 1) * C, 0, base:]
        for k in range(2 * nbd):
            codes[q, k] = jnp.broadcast_to(meta[:, k : k + 1], (C, bsz))

        def body(c, acc):
            for k in range(nbd):
                hit = rio == codes[q, k, pl.ds(c, 1), :]
                acc = jnp.maximum(acc, jnp.where(hit, g1[q * C + c, :, k * bsz : (k + 1) * bsz], 0.0))
            return acc

        peak = lax.fori_loop(0, C, body, jnp.zeros((rb, bsz), F32), unroll=min(C, 8))
        dr[q * rb : (q + 1) * rb, :] = 1.0 / jnp.sqrt(jnp.maximum(peak, 0.5))
    share = iota((C, bsz), 1) // (bsz // C)
    mine = jnp.full((C, bsz), -1.0, F32)
    for k in range(nbd):
        mine = jnp.where(share == k, codes[me_r, k], mine)
    packed[...] = mine
    top = jnp.zeros((cb, bsz), F32)
    groups = [origins(me_r, s) for s in range(half)]
    for q, slot in zip(groups, slots):
        at = pl.ds(pl.multiple_of(q * rb, rb), rb)
        w_ref[at, :] = dr[at, :] * slot[base : base + rb, :]
        top = jnp.maximum(top, col_peaks(nbd, cb, q, slot, codes))
    colmax[...] = top
    for s, (q, slot) in enumerate(zip(groups, slots)):
        split_blocks(nbd, slot, parts.at[s])
        part[q] = backward(nbd, rb, cb, q, parts.at[s], codes, w_ref)
    split_blocks(nbd, turned, own)


def primal_kernel(nbd, R, C, rb, cb, origins, *refs):
    half = R // 2 + 1 if R > 1 else 1
    slots, own = refs[: R - half], refs[R - half]
    aux, dr, codes, done, colmax, x_new, dc, p3, parts, w_ref, part = refs[R - half + 1 :]
    me_r = lax.axis_index("row")
    me_c = lax.axis_index("col")
    bsz = x_new.shape[1]
    base = nbd * bsz
    x_prev, cost, upper = (aux[i * cb : (i + 1) * cb, :] for i in range(3))
    eta, omega = (aux[3 * cb + i : 3 * cb + i + 1, :] for i in range(2))
    cio = iota((cb, bsz), 0).astype(F32)
    top = colmax[...]
    for s in range(half):
        q = origins(me_r, s)
        part[q] = done[q]
    groups = [origins(me_r, s) for s in range(half, R)]
    for q, slot in zip(groups, slots):
        at = pl.ds(pl.multiple_of(q * rb, rb), rb)
        w_ref[at, :] = dr[at, :] * slot[base : base + rb, :]
        top = jnp.maximum(top, col_peaks(nbd, cb, q, slot, codes))
    for s, (q, slot) in enumerate(zip(groups, slots)):
        split_blocks(nbd, slot, parts.at[s])
        part[q] = backward(nbd, rb, cb, q, parts.at[s], codes, w_ref)
    got = part[0]
    for q in range(1, R):
        got += part[q]
    scale = 1.0 / jnp.sqrt(jnp.maximum(top, 0.5))
    dc[...] = scale
    grad = scale * cost - got * scale
    xn = jnp.clip(x_prev - eta / omega * grad, 0.0, upper / scale)
    x_new[...] = xn
    v2 = scale * (xn - x_prev)
    v1 = 0.5 * (scale * xn) + 0.5 * v2
    sub = iota((up(2 * nbd, 8), bsz), 0)
    picks = []
    for k in range(nbd):
        hit = cio == codes[me_r, nbd + k, pl.ds(me_c, 1), :]
        one, two = (total(jnp.where(hit, v, 0.0)) for v in (v1, v2))
        picks.append(jnp.where(sub == k, one, jnp.where(sub == nbd + k, two, 0.0)))
    rows = product(jnp.concatenate(picks, axis=1), lambda i: own[i], ((1,), (0,)))
    lanes = bsz // C
    turn = (iota((C, bsz), 1) // lanes + iota((C, bsz), 0)) % C
    row = jnp.zeros((C, bsz), F32)
    for k in range(nbd):
        part_k = pltpu.roll(rows[nbd + k : nbd + k + 1, :], (k + 1) * lanes % bsz, 1)
        row = jnp.where(turn == k, part_k, row)
        p3[:, :, k * bsz : (k + 1) * bsz] = jnp.broadcast_to(
            rows[k : k + 1, :][None], (p3.shape[0], 1, bsz)
        )
    row = pltpu.roll(row, 0, 1, stride=lanes, stride_axis=0)
    for q in range(R):
        p3[q * C : (q + 1) * C, 0, base:] = row


def dual_kernel(nbd, R, C, rb, cb, origins, g3, *refs):
    slots = refs[:R]
    early, late, aux, dr, codes, packed, x_new, dc, y_new, p4, dual, w_ref, part = refs[R:]
    me_r = lax.axis_index("row")
    me_c = lax.axis_index("col")
    bsz = x_new.shape[1]
    base = nbd * bsz
    x_prev, cost, upper = (aux[i * cb : (i + 1) * cb, :] for i in range(3))
    eta, omega = (aux[3 * cb + i : 3 * cb + i + 1, :] for i in range(2))
    rio = iota((rb, bsz), 0).astype(F32)
    sigma = eta * omega
    for s, slot in enumerate(slots):
        q = origins(me_r, s)
        at = pl.ds(pl.multiple_of(q * rb, rb), rb)

        def body(c, acc):
            for k in range(nbd):
                hit = rio == codes[q, k, pl.ds(c, 1), :]
                acc = acc + jnp.where(hit, g3[q * C + c, :, k * bsz : (k + 1) * bsz], 0.0)
            return acc

        both = lax.fori_loop(0, C, body, jnp.zeros((rb, bsz), F32), unroll=min(C, 8))
        scale = dr[at, :]
        both = both * (2.0 * scale)
        bs = scale * slot[base + rb : base + 2 * rb, :]
        yp = slot[base : base + rb, :]
        yn = yp + sigma * (bs - both)
        w_ref[at, :] = scale * yn
        dy = yn - yp
        part[q, 0:1, :] = total(dy * dy)
        part[q, 1:2, :] = total(bs * yn)
        if s == 0:
            y_new[...] = yn

            def mine(c, acc):
                hit = rio == packed[pl.ds(c, 1), :]
                return acc + jnp.where(hit, g3[q * C + c, :, base:], 0.0)

            shares = lax.fori_loop(0, C, mine, jnp.zeros((rb, bsz), F32), unroll=min(C, 8))
            lanes = bsz // C
            adx = shares
            for k in range(1, nbd):
                adx = adx + pltpu.roll(shares, bsz - k * lanes, 1)
            adx = pltpu.roll(adx, (C - 1 - me_c) * lanes, 1) * scale
            inside = iota((rb, bsz), 1) // lanes == C - 1 - me_c
            adx = jnp.where(inside, adx, 0.0)
            resid = jnp.where(inside, bs - (both - adx), 0.0)
            adx2 = total(adx * adx)
            res2 = total(resid * resid)
    sums = part[0, :2, :]
    for q in range(1, R):
        sums += part[q, :2, :]
    dual[:2, :] = jnp.broadcast_to(jnp.sum(sums, axis=1, keepdims=True), (2, bsz))
    dual[2:, :] = jnp.broadcast_to(omega, (6, bsz))
    groups = [origins(me_r, s) for s in range(R)]
    half = early.shape[0]
    for s, q in enumerate(groups):
        parts = early.at[s] if s < half else late.at[s - half]
        part[q] = backward(nbd, rb, cb, q, parts, codes, w_ref)
    got = part[0]
    for q in range(1, R):
        got += part[q]
    scale = dc[...]
    cs = scale * cost
    reduced = cs - got * scale
    us = upper / scale
    xn = x_new[...]
    dx = xn - x_prev
    terms = [total(dx * dx), total(cs * xn), total(us * jnp.maximum(-reduced, 0.0)), adx2, res2]
    sub, lane = iota((8, bsz), 0), iota((8, bsz), 1)
    stack = jnp.zeros((8, bsz), F32)
    for i, term in enumerate(terms):
        stack = jnp.where(sub == i, term, stack)
    sums = jnp.sum(stack, axis=1, keepdims=True)
    out = total(jnp.where(sub == lane, sums, 0.0))
    p4[...] = jnp.broadcast_to(out[None], p4.shape)


def stats_kernel(C, total_rows, total_cols, g4, dual, x_new, y_new, stats, x_out, y_out, last, sems):
    outs = [
        pltpu.make_async_copy(a, b, sems.at[i])
        for i, (a, b) in enumerate(((x_new, x_out), (y_new, y_out), (last, stats)))
    ]
    outs[0].start()
    outs[1].start()
    bsz = g4.shape[2]
    sums = g4[0]
    for c in range(1, C):
        sums += g4[c]
    every = sums
    for d in range(C, g4.shape[0]):
        every += g4[d]
    sub, lane = iota((8, bsz), 0), iota((8, bsz), 1)
    stack = jnp.where(lane < 3, sums, every)
    stack = jnp.broadcast_to(
        jnp.sum(jnp.where(sub == lane, stack, 0.0), axis=1, keepdims=True), (8, bsz)
    )
    dx2, cx, uneg, adx2, res2 = (stack[i : i + 1, :] for i in range(5))
    dy2, by = (dual[i : i + 1, :] for i in range(2))
    lane = lane[:1]
    omega = dual[2:3, :]
    movement = 0.5 * omega * dx2 + 0.5 / omega * dy2
    first = jnp.sqrt(res2 / total_rows)
    second = (cx - by + uneg) / total_cols
    third = movement / jnp.sqrt(adx2 * dy2 + 1e-06)
    out = jnp.where(lane == 0, first, jnp.where(lane == 1, second, third))
    last[...] = out[:, : last.shape[1]]
    outs[2].start()
    for copy in outs:
        copy.wait()


def shards(blocks, block_rows, block_cols, counts, x_prev, y_prev, cost, rhs, upper, steps):
    R = lax.axis_size("row")
    C = lax.axis_size("col")
    ndev = R * C
    nbd, bsz = blocks.shape[2], blocks.shape[3]
    rb = y_prev.shape[0] // bsz
    cb = x_prev.shape[0] // bsz
    half = R // 2 + 1 if R > 1 else 1
    in_hbm = functools.partial(pltpu.with_memory_space_constraint, memory_space=pltpu.HBM)
    shape = lambda *dims: jax.ShapeDtypeStruct(dims, F32)
    params = pltpu.CompilerParams(vmem_limit_bytes=LIMIT)
    raw = (
        blocks.reshape(nbd * bsz, bsz),
        y_prev.reshape(rb, bsz),
        rhs.reshape(rb, bsz),
        x_prev.reshape(cb, bsz),
        cost.reshape(cb, bsz),
        upper.reshape(cb, bsz),
        block_rows,
        block_cols,
        steps,
    )
    p1, bulk, aux, turned = pl.pallas_call(
        functools.partial(peaks_kernel, nbd),
        out_shape=(
            shape(ndev, 1, (nbd + 1) * bsz),
            shape(nbd * bsz + 2 * rb, bsz),
            shape(3 * cb + 8, bsz),
            shape(nbd * bsz, bsz),
        ),
        in_specs=[HBM] * len(raw) + [SMEM],
        out_specs=(VMEM,) * 4,
        scratch_shapes=[
            pltpu.SMEM((1, 1, nbd), jnp.int32),
            pltpu.SMEM((1, 1, nbd), jnp.int32),
            pltpu.SMEM(steps.shape, F32),
            pltpu.SemaphoreType.DMA((9,)),
        ],
        compiler_params=params,
        name="peaks",
    )(*map(in_hbm, raw), counts)

    def spread(v):
        return lax.all_to_all(v, ("row", "col"), 0, 0, tiled=True)

    def swap(v, step):
        return lax.ppermute(v, "row", [(i, i ^ step) for i in range(R)])

    far, far_ids, step = [bulk], [0], R // 2
    while step > 1:
        far += [swap(v, step) for v in far]
        far_ids += [i ^ step for i in far_ids]
        step //= 2
    slots, ids = far[:1], [0]
    if R > 1:
        slots.append(swap(bulk, 1))
        ids.append(1)
    g1 = spread(p1)
    g1, slots[-1], *far = lax.optimization_barrier((g1, slots[-1], *far[1:]))
    slots += far + [swap(v, 1) for v in far]
    ids += far_ids[1:] + [i ^ 1 for i in far_ids[1:]]

    def origins(me, s):
        return me ^ ids[s] if ids[s] else me

    scratch = [pltpu.VMEM((R * rb, bsz), F32)]

    def parts_of(n):
        return jax.ShapeDtypeStruct((n, SPLITS, nbd * bsz, bsz), jnp.bfloat16)

    part = pltpu.VMEM((R, up(cb, 8), bsz), F32)
    sizes = (nbd, R, C, rb, cb, origins)
    dr, codes, packed, done, colmax, early, own = pl.pallas_call(
        functools.partial(scales_kernel, *sizes),
        out_shape=(
            shape(R * rb, bsz),
            shape(R, 2 * nbd, C, bsz),
            shape(C, bsz),
            shape(R, cb, bsz),
            shape(cb, bsz),
            parts_of(half),
            jax.ShapeDtypeStruct((SPLITS, nbd * bsz, bsz), jnp.bfloat16),
        ),
        in_specs=[VMEM] * (2 + half),
        out_specs=(VMEM,) * 7,
        scratch_shapes=scratch,
        compiler_params=params,
        name="scales",
    )(g1, turned, *slots[:half])
    x_new, dc, p3, late = pl.pallas_call(
        functools.partial(primal_kernel, *sizes),
        out_shape=(
            shape(cb, bsz),
            shape(cb, bsz),
            shape(ndev, 1, (nbd + 1) * bsz),
            parts_of(max(R - half, 1)),
        ),
        in_specs=[VMEM] * (R - half + 6),
        out_specs=(VMEM,) * 4,
        scratch_shapes=scratch + [part],
        compiler_params=params,
        name="primal",
    )(*slots[half:], own, aux, dr, codes, done, colmax)
    g3 = spread(p3)
    y_new, p4, dual = pl.pallas_call(
        functools.partial(dual_kernel, *sizes),
        out_shape=(shape(rb, bsz), shape(ndev, 1, bsz), shape(8, bsz)),
        in_specs=[VMEM] * (R + 9),
        out_specs=(VMEM,) * 3,
        scratch_shapes=scratch + [part],
        compiler_params=params,
        name="dual",
    )(g3, *slots, early, late, aux, dr, codes, packed, x_new, dc)
    g4 = spread(p4)
    stats, x_new, y_new = pl.pallas_call(
        functools.partial(
            stats_kernel, C, float(y_prev.shape[0] * R), float(x_prev.shape[0] * C)
        ),
        out_shape=(shape(1, 3), shape(cb, bsz), shape(rb, bsz)),
        in_specs=[VMEM] * 4,
        out_specs=(HBM,) * 3,
        scratch_shapes=[pltpu.VMEM((1, 3), F32), pltpu.SemaphoreType.DMA((3,))],
        compiler_params=params,
        name="stats",
    )(g4, dual, x_new, y_new)
    return (x_new.reshape(-1), y_new.reshape(-1), stats.reshape(-1))


def solution(mesh):
    placed = (
        P("row", "col", None, None, None),
        P("row", "col", None),
        P("row", "col", None),
        P("row", "col"),
        P("col"),
        P("row"),
        P("col"),
        P("row"),
        P("col"),
        P(),
    )
    return jax.shard_map(
        shards, mesh=mesh, in_specs=placed, out_specs=(P("col"), P("row"), P()), check_vma=False
    )
```

```python
import functools

import jax
import jax.numpy as jnp
from jax import lax
from jax.experimental import pallas as pl
from jax.experimental.pallas import tpu as pltpu
from jax.sharding import PartitionSpec as P

F32 = jnp.float32
VMEM = pl.BlockSpec(memory_space=pltpu.VMEM)
SMEM = pl.BlockSpec(memory_space=pltpu.SMEM)
HBM = pl.BlockSpec(memory_space=pltpu.HBM)
LIMIT = 40 * 1024 * 1024
SPLITS = 3


def up(n, m):
    return -(-n // m) * m


def iota(shape, dim):
    return lax.broadcasted_iota(jnp.int32, shape, dim)


def total(rows):
    return jnp.sum(rows, axis=0, keepdims=True)


def peaks_kernel(nbd, blocks, y, rhs, x, cost, upper, brow, bcol, steps, count, p1, bulk, aux, turned, *scratch):
    s_row, s_col, s_steps, sems = scratch
    bsz = bulk.shape[1]
    rb = y.shape[0]
    cb = x.shape[0]
    base = nbd * bsz
    pairs = [
        (blocks, bulk.at[:base]),
        (brow, s_row),
        (bcol, s_col),
        (steps, s_steps),
        (y, bulk.at[base : base + rb]),
        (rhs, bulk.at[base + rb : base + 2 * rb]),
        (x, aux.at[:cb]),
        (cost, aux.at[cb : 2 * cb]),
        (upper, aux.at[2 * cb : 3 * cb]),
    ]
    loads = [pltpu.make_async_copy(a, b, sems.at[i]) for i, (a, b) in enumerate(pairs)]
    for copy in loads:
        copy.start()
    loads[0].wait()
    peaks = []
    for k in range(nbd):
        a = bulk[k * bsz : (k + 1) * bsz, :]
        a = a.T
        turned[k * bsz : (k + 1) * bsz, :] = a
        peaks.append(jnp.max(jnp.abs(a), axis=0, keepdims=True))
    for copy in loads[1:]:
        copy.wait()
    lane = iota((1, bsz), 1)
    meta = jnp.full((1, bsz), -1.0, F32)
    for k in range(nbd):
        code = jnp.where(k < count[0, 0], s_row[0, 0, k], -1).astype(F32)
        meta = jnp.where(lane == k, code, meta)
        meta = jnp.where(lane == nbd + k, s_col[0, 0, k].astype(F32), meta)
    for k, piece in enumerate(peaks + [meta]):
        p1[:, :, k * bsz : (k + 1) * bsz] = jnp.broadcast_to(piece[None], (p1.shape[0], 1, bsz))
    asub = iota((8, bsz), 0)
    aux[3 * cb :, :] = jnp.where(asub == 0, s_steps[0], s_steps[1])


def split(v):
    parts = []
    most = float(jnp.finfo(jnp.bfloat16).max)
    for _ in range(SPLITS):
        top = v if parts else jnp.clip(v, -most, most)
        top = top.astype(jnp.bfloat16).astype(F32)
        parts.append(top)
        v = v - top
    return parts


def split_blocks(nbd, slot, out):
    bsz = slot.shape[1]
    for k in range(nbd):
        at = slice(k * bsz, (k + 1) * bsz)
        for i, v in enumerate(split(slot[at, :])):
            out[i, at, :] = v.astype(jnp.bfloat16)


def product(left, right, dims):
    n = left.shape[0]
    left = jnp.concatenate(split(left), axis=0).astype(jnp.bfloat16)
    out = 0.0
    for j in range(SPLITS):
        got = lax.dot_general(left, right(j), (dims, ((), ())), preferred_element_type=F32)
        for i in range(SPLITS - j):
            out = out + got[i * n : (i + 1) * n]
    return out


def pick(nbd, q, codes, values):
    me_c = lax.axis_index("col")
    rio = iota(values.shape, 0).astype(F32)
    return [
        total(jnp.where(rio == codes[q, k, pl.ds(me_c, 1), :], values, 0.0)) for k in range(nbd)
    ]


def backward(nbd, cb, q, parts, codes, rows):
    me_c = lax.axis_index("col")
    cio = iota((cb, rows[0].shape[1]), 0).astype(F32)
    picks = [
        jnp.where(cio == codes[q, nbd + k, pl.ds(me_c, 1), :], rows[k], 0.0) for k in range(nbd)
    ]
    return product(jnp.concatenate(picks, axis=1), lambda i: parts[i], ((1,), (0,)))


def col_peaks(nbd, cb, q, slot, codes):
    me_c = lax.axis_index("col")
    bsz = slot.shape[1]
    cio = iota((cb, bsz), 0).astype(F32)
    out = jnp.zeros((cb, bsz), F32)
    for k in range(nbd):
        peak = jnp.max(jnp.abs(slot[k * bsz : (k + 1) * bsz, :]), axis=0, keepdims=True)
        live = codes[q, k, pl.ds(me_c, 1), :] >= 0.0
        hit = (cio == codes[q, nbd + k, pl.ds(me_c, 1), :]) & live
        out = jnp.maximum(out, jnp.where(hit, peak, 0.0))
    return out


def scales_kernel(nbd, R, C, rb, cb, origins, g1, turned, *refs):
    half = R // 2 + 1 if R > 1 else 1
    slots = refs[:half]
    dr, codes, packed, part, colmax, parts, own, w_ref = refs[half:]
    me_r = lax.axis_index("row")
    bsz = dr.shape[1]
    base = nbd * bsz
    rio = iota((rb, bsz), 0).astype(F32)
    for q in range(R):
        meta = g1[q * C : (q + 1) * C, 0, base:]
        for k in range(2 * nbd):
            codes[q, k] = jnp.broadcast_to(meta[:, k : k + 1], (C, bsz))

        def body(c, acc):
            for k in range(nbd):
                hit = rio == codes[q, k, pl.ds(c, 1), :]
                acc = jnp.maximum(acc, jnp.where(hit, g1[q * C + c, :, k * bsz : (k + 1) * bsz], 0.0))
            return acc

        peak = lax.fori_loop(0, C, body, jnp.zeros((rb, bsz), F32), unroll=min(C, 8))
        dr[q * rb : (q + 1) * rb, :] = 1.0 / jnp.sqrt(jnp.maximum(peak, 0.5))
    share = iota((C, bsz), 1) // (bsz // C)
    mine = jnp.full((C, bsz), -1.0, F32)
    for k in range(nbd):
        mine = jnp.where(share == k, codes[me_r, k], mine)
    packed[...] = mine
    top = jnp.zeros((cb, bsz), F32)
    groups = [origins(me_r, s) for s in range(half)]
    for q, slot in zip(groups, slots):
        at = pl.ds(pl.multiple_of(q * rb, rb), rb)
        w_ref[at, :] = dr[at, :] * slot[base : base + rb, :]
        top = jnp.maximum(top, col_peaks(nbd, cb, q, slot, codes))
    colmax[...] = top
    for s, (q, slot) in enumerate(zip(groups, slots)):
        split_blocks(nbd, slot, parts.at[s])
        part[q] = backward(nbd, cb, q, parts.at[s], codes, pick(nbd, q, codes, w_ref[pl.ds(pl.multiple_of(q * rb, rb), rb), :]))
    split_blocks(nbd, turned, own)


def primal_kernel(nbd, R, C, rb, cb, origins, *refs):
    half = R // 2 + 1 if R > 1 else 1
    slots, own = refs[: R - half], refs[R - half]
    aux, dr, codes, done, colmax, x_new, dc, p3, parts, w_ref, part = refs[R - half + 1 :]
    me_r = lax.axis_index("row")
    me_c = lax.axis_index("col")
    bsz = x_new.shape[1]
    base = nbd * bsz
    x_prev, cost, upper = (aux[i * cb : (i + 1) * cb, :] for i in range(3))
    eta, omega = (aux[3 * cb + i : 3 * cb + i + 1, :] for i in range(2))
    cio = iota((cb, bsz), 0).astype(F32)
    top = colmax[...]
    for s in range(half):
        q = origins(me_r, s)
        part[q] = done[q]
    groups = [origins(me_r, s) for s in range(half, R)]
    for q, slot in zip(groups, slots):
        at = pl.ds(pl.multiple_of(q * rb, rb), rb)
        w_ref[at, :] = dr[at, :] * slot[base : base + rb, :]
        top = jnp.maximum(top, col_peaks(nbd, cb, q, slot, codes))
    for s, (q, slot) in enumerate(zip(groups, slots)):
        split_blocks(nbd, slot, parts.at[s])
        part[q] = backward(nbd, cb, q, parts.at[s], codes, pick(nbd, q, codes, w_ref[pl.ds(pl.multiple_of(q * rb, rb), rb), :]))
    got = part[0]
    for q in range(1, R):
        got += part[q]
    scale = 1.0 / jnp.sqrt(jnp.maximum(top, 0.5))
    dc[...] = scale
    grad = scale * cost - got * scale
    xn = jnp.clip(x_prev - eta / omega * grad, 0.0, upper / scale)
    x_new[...] = xn
    v2 = scale * (xn - x_prev)
    v1 = 0.5 * (scale * xn) + 0.5 * v2
    sub = iota((up(2 * nbd, 8), bsz), 0)
    picks = []
    for k in range(nbd):
        hit = cio == codes[me_r, nbd + k, pl.ds(me_c, 1), :]
        one, two = (total(jnp.where(hit, v, 0.0)) for v in (v1, v2))
        picks.append(jnp.where(sub == k, one, jnp.where(sub == nbd + k, two, 0.0)))
    rows = product(jnp.concatenate(picks, axis=1), lambda i: own[i], ((1,), (0,)))
    lanes = bsz // C
    turn = (iota((C, bsz), 1) // lanes + iota((C, bsz), 0)) % C
    row = jnp.zeros((C, bsz), F32)
    for k in range(nbd):
        part_k = pltpu.roll(rows[nbd + k : nbd + k + 1, :], (k + 1) * lanes % bsz, 1)
        row = jnp.where(turn == k, part_k, row)
        p3[:, :, k * bsz : (k + 1) * bsz] = jnp.broadcast_to(
            rows[k : k + 1, :][None], (p3.shape[0], 1, bsz)
        )
    row = pltpu.roll(row, 0, 1, stride=lanes, stride_axis=0)
    for q in range(R):
        p3[q * C : (q + 1) * C, 0, base:] = row


def dual_kernel(nbd, R, C, rb, cb, origins, g3, *refs):
    slots = refs[:R]
    early, late, aux, dr, codes, packed, x_new, dc, y_new, p4, dual, part = refs[R:]
    me_r = lax.axis_index("row")
    me_c = lax.axis_index("col")
    bsz = x_new.shape[1]
    base = nbd * bsz
    x_prev, cost, upper = (aux[i * cb : (i + 1) * cb, :] for i in range(3))
    eta, omega = (aux[3 * cb + i : 3 * cb + i + 1, :] for i in range(2))
    rio = iota((rb, bsz), 0).astype(F32)
    sigma = eta * omega
    half = early.shape[0]
    for s, slot in enumerate(slots):
        q = origins(me_r, s)
        scale = dr[pl.ds(pl.multiple_of(q * rb, rb), rb), :]
        bs = scale * slot[base + rb : base + 2 * rb, :]
        yp = slot[base : base + rb, :]
        if s == 0:

            def body(c, acc):
                for k in range(nbd):
                    hit = rio == codes[q, k, pl.ds(c, 1), :]
                    acc = acc + jnp.where(hit, g3[q * C + c, :, k * bsz : (k + 1) * bsz], 0.0)
                return acc

            def mine(c, acc):
                hit = rio == packed[pl.ds(c, 1), :]
                return acc + jnp.where(hit, g3[q * C + c, :, base:], 0.0)

            zero = jnp.zeros((rb, bsz), F32)
            both = lax.fori_loop(0, C, body, zero, unroll=min(C, 8)) * (2.0 * scale)
            shares = lax.fori_loop(0, C, mine, zero, unroll=min(C, 8))
            yn = yp + sigma * (bs - both)
            y_new[...] = yn
            rows = pick(nbd, q, codes, scale * yn)
            dy = yn - yp
            dy2, by = total(dy * dy), total(bs * yn)
            lanes = bsz // C
            adx = shares
            for k in range(1, nbd):
                adx = adx + pltpu.roll(shares, bsz - k * lanes, 1)
            adx = pltpu.roll(adx, (C - 1 - me_c) * lanes, 1) * scale
            inside = iota((rb, bsz), 1) // lanes == C - 1 - me_c
            adx = jnp.where(inside, adx, 0.0)
            resid = jnp.where(inside, bs - (both - adx), 0.0)
            adx2, res2 = total(adx * adx), total(resid * resid)
        else:
            at = pl.ds(q * C, C)
            got = [g3[at, 0, k * bsz : (k + 1) * bsz] for k in range(nbd)]
            still = pick(nbd, q, codes, yp + sigma * bs)
            scales = pick(nbd, q, codes, scale)
            rows = []
            for k in range(nbd):
                code = codes[q, k, pl.ds(me_c, 1), :]
                both = jnp.zeros((C, bsz), F32)
                for j in range(nbd):
                    both = both + jnp.where(codes[q, j] == code, got[j], 0.0)
                row = scales[k] * (still[k] - sigma * (total(both) * (2.0 * scales[k])))
                rows.append(jnp.where(code >= 0.0, row, 0.0))
        parts = early.at[s] if s < half else late.at[s - half]
        part[q] = backward(nbd, cb, q, parts, codes, rows)
    dual[...] = jnp.broadcast_to(omega, dual.shape)
    got = part[0]
    for q in range(1, R):
        got += part[q]
    scale = dc[...]
    cs = scale * cost
    reduced = cs - got * scale
    us = upper / scale
    xn = x_new[...]
    dx = xn - x_prev
    terms = [total(dx * dx), total(cs * xn), total(us * jnp.maximum(-reduced, 0.0)), adx2, res2, dy2, by]
    sub, lane = iota((8, bsz), 0), iota((8, bsz), 1)
    stack = jnp.zeros((8, bsz), F32)
    for i, term in enumerate(terms):
        stack = jnp.where(sub == i, term, stack)
    sums = jnp.sum(stack, axis=1, keepdims=True)
    out = total(jnp.where(sub == lane, sums, 0.0))
    p4[...] = jnp.broadcast_to(out[None], p4.shape)


def stats_kernel(C, total_rows, total_cols, g4, dual, x_new, y_new, stats, x_out, y_out, last, sems):
    outs = [
        pltpu.make_async_copy(a, b, sems.at[i])
        for i, (a, b) in enumerate(((x_new, x_out), (y_new, y_out), (last, stats)))
    ]
    outs[0].start()
    outs[1].start()
    bsz = g4.shape[2]
    sums = g4[0]
    for c in range(1, C):
        sums += g4[c]
    groups = g4[0]
    for q in range(1, g4.shape[0] // C):
        groups += g4[q * C]
    every = sums
    for d in range(C, g4.shape[0]):
        every += g4[d]
    sub, lane = iota((8, bsz), 0), iota((8, bsz), 1)
    stack = jnp.where(lane < 3, sums, jnp.where(lane < 5, every, groups))
    stack = jnp.broadcast_to(
        jnp.sum(jnp.where(sub == lane, stack, 0.0), axis=1, keepdims=True), (8, bsz)
    )
    dx2, cx, uneg, adx2, res2, dy2, by = (stack[i : i + 1, :] for i in range(7))
    lane = lane[:1]
    omega = dual[:1, :]
    movement = 0.5 * omega * dx2 + 0.5 / omega * dy2
    first = jnp.sqrt(res2 / total_rows)
    second = (cx - by + uneg) / total_cols
    third = movement / jnp.sqrt(adx2 * dy2 + 1e-06)
    out = jnp.where(lane == 0, first, jnp.where(lane == 1, second, third))
    last[...] = out[:, : last.shape[1]]
    outs[2].start()
    for copy in outs:
        copy.wait()


def shards(blocks, block_rows, block_cols, counts, x_prev, y_prev, cost, rhs, upper, steps):
    R = lax.axis_size("row")
    C = lax.axis_size("col")
    ndev = R * C
    nbd, bsz = blocks.shape[2], blocks.shape[3]
    rb = y_prev.shape[0] // bsz
    cb = x_prev.shape[0] // bsz
    half = R // 2 + 1 if R > 1 else 1
    in_hbm = functools.partial(pltpu.with_memory_space_constraint, memory_space=pltpu.HBM)
    shape = lambda *dims: jax.ShapeDtypeStruct(dims, F32)
    params = pltpu.CompilerParams(vmem_limit_bytes=LIMIT)
    raw = (
        blocks.reshape(nbd * bsz, bsz),
        y_prev.reshape(rb, bsz),
        rhs.reshape(rb, bsz),
        x_prev.reshape(cb, bsz),
        cost.reshape(cb, bsz),
        upper.reshape(cb, bsz),
        block_rows,
        block_cols,
        steps,
    )
    p1, bulk, aux, turned = pl.pallas_call(
        functools.partial(peaks_kernel, nbd),
        out_shape=(
            shape(ndev, 1, (nbd + 1) * bsz),
            shape(nbd * bsz + 2 * rb, bsz),
            shape(3 * cb + 8, bsz),
            shape(nbd * bsz, bsz),
        ),
        in_specs=[HBM] * len(raw) + [SMEM],
        out_specs=(VMEM,) * 4,
        scratch_shapes=[
            pltpu.SMEM((1, 1, nbd), jnp.int32),
            pltpu.SMEM((1, 1, nbd), jnp.int32),
            pltpu.SMEM(steps.shape, F32),
            pltpu.SemaphoreType.DMA((9,)),
        ],
        compiler_params=params,
        name="peaks",
    )(*map(in_hbm, raw), counts)

    def spread(v):
        return lax.all_to_all(v, ("row", "col"), 0, 0, tiled=True)

    def swap(v, step):
        return lax.ppermute(v, "row", [(i, i ^ step) for i in range(R)])

    far, far_ids, step = [bulk], [0], R // 2
    while step > 1:
        far += [swap(v, step) for v in far]
        far_ids += [i ^ step for i in far_ids]
        step //= 2
    slots, ids = far[:1], [0]
    if R > 1:
        slots.append(swap(bulk, 1))
        ids.append(1)
    g1 = spread(p1)
    g1, slots[-1], *far = lax.optimization_barrier((g1, slots[-1], *far[1:]))
    slots += far + [swap(v, 1) for v in far]
    ids += far_ids[1:] + [i ^ 1 for i in far_ids[1:]]

    def origins(me, s):
        return me ^ ids[s] if ids[s] else me

    scratch = [pltpu.VMEM((R * rb, bsz), F32)]

    def parts_of(n):
        return jax.ShapeDtypeStruct((n, SPLITS, nbd * bsz, bsz), jnp.bfloat16)

    part = pltpu.VMEM((R, up(cb, 8), bsz), F32)
    sizes = (nbd, R, C, rb, cb, origins)
    dr, codes, packed, done, colmax, early, own = pl.pallas_call(
        functools.partial(scales_kernel, *sizes),
        out_shape=(
            shape(R * rb, bsz),
            shape(R, 2 * nbd, C, bsz),
            shape(C, bsz),
            shape(R, cb, bsz),
            shape(cb, bsz),
            parts_of(half),
            jax.ShapeDtypeStruct((SPLITS, nbd * bsz, bsz), jnp.bfloat16),
        ),
        in_specs=[VMEM] * (2 + half),
        out_specs=(VMEM,) * 7,
        scratch_shapes=scratch,
        compiler_params=params,
        name="scales",
    )(g1, turned, *slots[:half])
    x_new, dc, p3, late = pl.pallas_call(
        functools.partial(primal_kernel, *sizes),
        out_shape=(
            shape(cb, bsz),
            shape(cb, bsz),
            shape(ndev, 1, (nbd + 1) * bsz),
            parts_of(max(R - half, 1)),
        ),
        in_specs=[VMEM] * (R - half + 6),
        out_specs=(VMEM,) * 4,
        scratch_shapes=scratch + [part],
        compiler_params=params,
        name="primal",
    )(*slots[half:], own, aux, dr, codes, done, colmax)
    g3 = spread(p3)
    y_new, p4, dual = pl.pallas_call(
        functools.partial(dual_kernel, *sizes),
        out_shape=(shape(rb, bsz), shape(ndev, 1, bsz), shape(8, bsz)),
        in_specs=[VMEM] * (R + 9),
        out_specs=(VMEM,) * 3,
        scratch_shapes=[part],
        compiler_params=params,
        name="dual",
    )(g3, *slots, early, late, aux, dr, codes, packed, x_new, dc)
    g4 = spread(p4)
    stats, x_new, y_new = pl.pallas_call(
        functools.partial(
            stats_kernel, C, float(y_prev.shape[0] * R), float(x_prev.shape[0] * C)
        ),
        out_shape=(shape(1, 3), shape(cb, bsz), shape(rb, bsz)),
        in_specs=[VMEM] * 4,
        out_specs=(HBM,) * 3,
        scratch_shapes=[pltpu.VMEM((1, 3), F32), pltpu.SemaphoreType.DMA((3,))],
        compiler_params=params,
        name="stats",
    )(g4, dual, x_new, y_new)
    return (x_new.reshape(-1), y_new.reshape(-1), stats.reshape(-1))


def solution(mesh):
    placed = (
        P("row", "col", None, None, None),
        P("row", "col", None),
        P("row", "col", None),
        P("row", "col"),
        P("col"),
        P("row"),
        P("col"),
        P("row"),
        P("col"),
        P(),
    )
    return jax.shard_map(
        shards, mesh=mesh, in_specs=placed, out_specs=(P("col"), P("row"), P()), check_vma=False
    )
```
